512 devices in a mesh: kt: 128 (over x, y, z_lo, core), en: 4 (over z_hi).
Axes of the slice: x: 4, y: 4, z: 16 (z_hi: 4, z_lo: 4; z = z_hi * 4 + z_lo), core: 2. Of those that a mesh axis runs over, the one named last changes fastest.
Arguments:
- counts: int32 [128], P('kt'), may hold values from 1 to 4, 256 in all
- contact_slabs: int32 [2], replicated, may hold values from 0 to 15
- onsite: float32 [16, 384], P('en'), may hold values from -0.5 to 0.5
- hopping: float32 [16, 384], P('en'), may hold values from 0.1 to 0.5
- potential_in: float32 [16, 384], P('en'), may hold values from -2 to 2
- couple_base: bfloat16 [16, 384, 384], P('en'), may hold values from -0.25 to 0.25
- couple_wave: bfloat16 [16, 384, 384], P('en'), may hold values from -0.25 to 0.25
- doping: float32 [16, 384], P('en'), may hold values from 0 to 2
- poisson_inverse: float32 [384, 384], replicated, may hold values from -0.3125 to 0.3125
Outputs:
- electron_populace: float32 [16, 384], P('en')
- potential_out: float32 [16, 384], P('en')
The draws below stay inside these ranges and needn't reach their ends.
Inputs may be any that keep to these rules, and one draw needn't show every extreme that they name: counts sum to 256 and the largest is 4.
All inputs are finite; a program needn't handle non-finite values. No bound on the sum of `counts` on one device may be relied on, other than what follows from the above.
Results may differ from the reference program's by a relative error of at most 0.00045.
Values may be sent and summed in bfloat16 or wider, within the bound.
A program may use at most 64 MiB of HBM per device.

```python
import math
import jax
import jax.numpy as jnp
import numpy as np
from jax import lax

ORB = 384
EMAX = 4
SLABS = 16
CROSS_IMPULSES = 128
LIVE = 256


def steps_of(stream_key, extent, cuts, smallest, high):
    def one(dim, parts):
        steps = jax.random.uniform(jax.random.fold_in(jax.random.fold_in(stream_key, 6), dim), (parts,), jnp.float32, smallest / len(cuts), high / len(cuts))
        return jnp.repeat(jnp.exp(steps), extent[dim] // parts).reshape((-1,) + (1,) * (len(extent) - dim - 1))

    loudness = one(*cuts[0])
    for cut in cuts[1:]:
        loudness = loudness * one(*cut)
    return loudness


def split_up(count, total, reach, skew):
    weights = [(1 << 20) // math.isqrt(rank ** skew) + 1 for rank in range(2, count + 1)]
    rest, holding = total - reach - (count - 1), [1] * (count - 1)
    while rest > 0:
        free = [i for i in range(count - 1) if holding[i] < reach]
        pool, remaining = sum([weights[i] for i in free]), rest
        for i in free:
            addition = min(reach - holding[i], max(1, remaining * weights[i] // pool), rest)
            holding[i] = holding[i] + addition
            rest = rest - addition
    return np.array([reach] + holding)


def uneven_parts(rng, number_of, total, limit, lean):
    if number_of == 2:
        one = jax.random.randint(rng, (), max(1, total - limit), min(limit, total - 1) + 1)
        return jnp.stack([one, total - one])
    sizes = jnp.asarray(split_up(number_of, total, limit, lean), jnp.int32)
    couples = (number_of - 1) // 2
    source_of, taker = sizes[1:1 + 2 * couples:2], sizes[2:2 + 2 * couples:2]
    room = jnp.minimum(source_of - 1, limit - taker)
    moved = jax.random.randint(jax.random.fold_in(rng, 1), (couples,), 0, 1 << 20) % (room + 1)
    sizes = sizes.at[1:1 + 2 * couples:2].set(source_of - moved).at[2:2 + 2 * couples:2].set(taker + moved)
    return sizes[jax.random.permutation(jax.random.fold_in(rng, 2), number_of)]


def centred(rng, shape, width, limit, split=(), kind=jnp.bfloat16):
    level = steps_of(rng, shape, split, -0.22, 0.18) if split else 1.0
    entries = jax.random.normal(rng, shape, jnp.float32) * width * level
    return jnp.minimum(jnp.maximum(entries, -limit), limit).astype(kind)


def setup_inputs(seed: int = 0) -> dict:
    arg_keys = jax.random.split(jax.random.key(seed), 10)
    return {
        "counts": uneven_parts(arg_keys[0], CROSS_IMPULSES, 2 * CROSS_IMPULSES, EMAX, 2).astype(jnp.int32),
        "contact_slabs": jax.random.randint(arg_keys[1], (2,), 0, SLABS).astype(jnp.int32),
        "onsite": jnp.clip(jax.random.uniform(arg_keys[2], (SLABS, ORB), jnp.float32, -0.5, 0.5) * steps_of(arg_keys[2], (SLABS, ORB), ((0, 4),), -0.4, 0.0), -0.5, 0.5),
        "hopping": jnp.clip(0.1 + 0.4 * jax.random.uniform(arg_keys[3], (SLABS, ORB), jnp.float32) ** steps_of(arg_keys[3], (SLABS, ORB), ((0, 4),), -0.2, 0.2), 0.1, 0.5),
        "potential_in": centred(arg_keys[4], (SLABS, ORB), 0.3, 2.0, ((0, 4),), jnp.float32),
        "couple_base": centred(arg_keys[5], (SLABS, ORB, ORB), (5 * ORB // 3) ** -0.5, 0.25, ((0, 4),)),
        "couple_wave": centred(arg_keys[6], (SLABS, ORB, ORB), (5 * ORB // 3) ** -0.5, 0.25, ((0, 4),)),
        "doping": jnp.clip(2.0 * jax.random.uniform(arg_keys[7], (SLABS, ORB), jnp.float32) ** steps_of(arg_keys[7], (SLABS, ORB), ((0, 4),), -0.2, 0.2), 0.0, 2.0),
        "poisson_inverse": centred(arg_keys[8], (ORB, ORB), ORB ** -0.5, 0.3125, (), jnp.float32),
    }


bottom_sample_mark = -1.0
sample_gap = 0.25
electrode_filling = -0.5
boltzmann_spread = 0.1
broadening = 1.0
contact_width = 0.5


def item_tables(counts, first_index, number):
    include_endpoint = jnp.cumsum(counts).astype(jnp.int32)
    exclusive = include_endpoint - counts
    item_index = first_index + jnp.arange(number, dtype=jnp.int32)
    transverse_impulse = jnp.sum((include_endpoint[None, :] <= item_index[:, None]).astype(jnp.int32), axis=1)
    selector = (jnp.arange(counts.shape[0], dtype=jnp.int32)[None, :] == transverse_impulse[:, None]).astype(jnp.int32)
    eigen_height = item_index - jnp.sum(selector * exclusive[None, :], axis=1)
    return transverse_impulse, eigen_height


def entry_amounts(transverse_impulse, eigen_height, impulse_count):
    wave_vector_number = jnp.pi * (transverse_impulse.astype(jnp.float32) + 0.5) / impulse_count
    angular_projection = jnp.cos(wave_vector_number)
    occupancy_mark = bottom_sample_mark + sample_gap * eigen_height.astype(jnp.float32)
    summation_multiplier = sample_gap / (1.0 + jnp.exp((occupancy_mark - electrode_filling) / boltzmann_spread)) / jnp.pi
    return angular_projection, occupancy_mark, summation_multiplier


def slab_step(carried, couple_base, couple_wave, angular_projection, diag_real, diag_imag):
    coupled = (couple_base.astype(jnp.float32) + angular_projection * couple_wave.astype(jnp.float32)).astype(jnp.bfloat16)
    left_part = jnp.einsum("rm,pmn->prn", coupled.astype(jnp.float32), carried.astype(jnp.float32)).astype(jnp.bfloat16)
    self_energy = jnp.einsum("prn,cn->prc", left_part.astype(jnp.float32), coupled.astype(jnp.float32))
    magnitude = diag_real * diag_real + diag_imag * diag_imag
    inv_real = diag_real / magnitude
    inv_imag = -diag_imag / magnitude
    half_real = inv_real[:, None] * self_energy[0] - inv_imag[:, None] * self_energy[1]
    half_imag = inv_real[:, None] * self_energy[1] + inv_imag[:, None] * self_energy[0]
    identity = jnp.eye(diag_real.shape[0], dtype=jnp.float32)
    green_real = half_real * inv_real[None, :] - half_imag * inv_imag[None, :] + identity * inv_real[None, :]
    green_imag = half_real * inv_imag[None, :] + half_imag * inv_real[None, :] + identity * inv_imag[None, :]
    return jnp.stack([green_real, green_imag]).astype(jnp.bfloat16), -jnp.diagonal(green_imag)


def reference(counts, contact_slabs, onsite, hopping, potential_in, couple_base, couple_wave, doping, poisson_inverse):
    transverse_impulse, eigen_height = item_tables(counts, 0, LIVE)
    angular_projection, occupancy_mark, summation_multiplier = entry_amounts(transverse_impulse, eigen_height, CROSS_IMPULSES)
    slab_ids = jnp.arange(SLABS, dtype=jnp.int32)
    contact_flag = jnp.any(slab_ids[:, None] == contact_slabs[None, :], axis=1).astype(jnp.float32)
    diag_imag = broadening + contact_width * contact_flag
    real_base = -onsite - potential_in

    def each_entry_share(values):
        item_cos, item_energy, item_weight = values
        carried = jnp.zeros((2, ORB, ORB), jnp.bfloat16)
        slab_rows = []
        for slab_index in range(SLABS):
            diag_real = item_energy + real_base[slab_index] - item_cos * hopping[slab_index]
            imag_row = jnp.full((ORB,), 1.0, jnp.float32) * diag_imag[slab_index]
            carried, diag_part = slab_step(carried, couple_base[slab_index], couple_wave[slab_index], item_cos, diag_real, imag_row)
            slab_rows.append(item_weight * diag_part)
        return jnp.stack(slab_rows)

    electron_populace = jnp.sum(lax.map(each_entry_share, (angular_projection, occupancy_mark, summation_multiplier)), axis=0)
    potential_out = jnp.dot(electron_populace - doping, poisson_inverse.T, precision=lax.Precision.HIGHEST)
    return electron_populace, potential_out
```

```python
import functools
import jax, jax.numpy as jnp
from jax import lax
from jax.experimental import pallas as pl
from jax.experimental.pallas import tpu as pltpu
from jax.sharding import PartitionSpec as P

NT = (((1,), (1,)), ((), ()))
f32, bf16 = jnp.float32, jnp.bfloat16

def chain_kernel(sym, scal_ref, tab_ref, w_ref, out_ref, g_ref, l_ref, c_ref):
    s = pl.program_id(0)
    n = w_ref.shape[-1]
    nb = n // 128
    cos, energy, weight = scal_ref[0], scal_ref[1], scal_ref[2]
    row = tab_ref[0]
    dr = energy + row[0:1] - cos * row[1:2]
    di = row[2:3]
    mag = dr * dr + di * di
    br = dr / mag
    bi = -di / mag
    eye = lax.broadcasted_iota(jnp.int32, (128, 128), 0) == lax.broadcasted_iota(jnp.int32, (128, 128), 1)
    brc = jnp.transpose(jnp.broadcast_to(br, (128, n)))
    bic = jnp.transpose(jnp.broadcast_to(bi, (128, n)))

    @pl.when(s == 0)
    def _():
        g_ref[...] = jnp.zeros_like(g_ref)
        for i in range(nb):
            sl = slice(128 * i, 128 * i + 128)
            g_ref[256 * i:256 * i + 128, sl] = jnp.where(eye, br[:, sl], 0.0).astype(bf16)
            g_ref[256 * i + 128:256 * i + 256, sl] = jnp.where(eye, bi[:, sl], 0.0).astype(bf16)
        out_ref[0] = -weight * bi

    @pl.when(s > 0)
    def _():
        c_ref[...] = (w_ref[0].astype(f32) + cos * w_ref[1].astype(f32)).astype(bf16)
        c = c_ref[...]
        for j in range(nb):
            L = lax.dot_general(c, g_ref[256 * j:256 * j + 256, :], NT, preferred_element_type=f32).astype(bf16)
            for i in range(nb):
                l_ref[256 * i:256 * i + 128, 128 * j:128 * j + 128] = L[128 * i:128 * i + 128, 0:128]
                l_ref[256 * i + 128:256 * i + 256, 128 * j:128 * j + 128] = L[128 * i:128 * i + 128, 128:256]
        for j in range(nb):
            lo = 128 * j if sym else 0
            sl = slice(128 * j, 128 * j + 128)
            SE = lax.dot_general(c_ref[lo:, :], l_ref[256 * j:256 * j + 256, :], NT, preferred_element_type=f32)
            for i in range(lo // 128, nb):
                se_r, se_i = SE[128 * i - lo:128 * i - lo + 128, :128], SE[128 * i - lo:128 * i - lo + 128, 128:]
                cr, ci = brc[128 * i:128 * i + 128], bic[128 * i:128 * i + 128]
                hr = cr * se_r - ci * se_i
                hi = cr * se_i + ci * se_r
                rr, ri = br[:, sl], bi[:, sl]
                gr = hr * rr - hi * ri
                gi = hr * ri + hi * rr
                if i == j:
                    gr = gr + jnp.where(eye, rr, 0.0)
                    gi = gi + jnp.where(eye, ri, 0.0)
                    out_ref[0, :, sl] = -weight * jnp.sum(jnp.where(eye, gi, 0.0), axis=0, keepdims=True)
                gr, gi = gr.astype(bf16), gi.astype(bf16)
                g_ref[256 * i:256 * i + 128, sl] = gr
                g_ref[256 * i + 128:256 * i + 256, sl] = gi
                if sym and i > j:
                    si = slice(128 * i, 128 * i + 128)
                    g_ref[256 * j:256 * j + 128, si] = jnp.transpose(gr)
                    g_ref[256 * j + 128:256 * j + 256, si] = jnp.transpose(gi)

def chain(scal, tab, w, sym=False):
    S, n = w.shape[0], w.shape[-1]
    return pl.pallas_call(
        functools.partial(chain_kernel, sym),
        grid=(S,),
        in_specs=[
            pl.BlockSpec(memory_space=pltpu.SMEM),
            pl.BlockSpec((1, 3, n), lambda s: (s, 0, 0)),
            pl.BlockSpec((None, 2, n, n), lambda s: (s, 0, 0, 0)),
        ],
        out_specs=pl.BlockSpec((1, 1, n), lambda s: (s, 0, 0)),
        out_shape=jax.ShapeDtypeStruct((S, 1, n), f32),
        scratch_shapes=[pltpu.VMEM((2 * n, n), bf16), pltpu.VMEM((2 * n, n), bf16), pltpu.VMEM((n, n), bf16)],
        compiler_params=pltpu.CompilerParams(vmem_limit_bytes=48 * 2**20),
    )(scal, tab, w)


ENERGIES = 4
BOTTOM, GAP, FILLING, SPREAD = -1.0, 0.25, -0.5, 0.1
BROADENING, CONTACT = 1.0, 0.5


def body(counts, contact_slabs, onsite, hopping, potential_in, couple_base, couple_wave, doping, poisson_inverse):
    kt_size, en_size = lax.axis_size("kt"), lax.axis_size("en")
    q, e = lax.axis_index("kt"), lax.axis_index("en")
    slabs, n = onsite.shape
    cos = jnp.cos(jnp.pi * (q.astype(f32) + 0.5) / kt_size)
    energy = BOTTOM + GAP * e.astype(f32)
    weight = GAP / (1.0 + jnp.exp((energy - FILLING) / SPREAD)) / jnp.pi
    weight = jnp.where(e < counts[0], weight, 0.0)
    slab_ids = e * slabs + jnp.arange(slabs, dtype=jnp.int32)
    contact = jnp.any(slab_ids[:, None] == contact_slabs[None, :], axis=1).astype(f32)
    imag = jnp.broadcast_to((BROADENING + CONTACT * contact)[:, None], (slabs, n))
    tab = lax.all_gather(jnp.stack([-onsite - potential_in, hopping, imag], 1), "en", tiled=True)
    rows = slabs * 2 * n // kt_size
    per = n // rows
    which = lax.rem(q // per, 2)
    place = (q // (2 * per), lax.rem(q, per) * rows, 0)
    piece = jnp.where(which == 0, lax.dynamic_slice(couple_base, place, (1, rows, n)),
                      lax.dynamic_slice(couple_wave, place, (1, rows, n)))[0]
    w = lax.all_gather(piece, ("kt", "en"), tiled=True).reshape(slabs, 2 * per, en_size, rows, n)
    w = w.transpose(2, 0, 1, 3, 4).reshape(slabs * en_size, 2, n, n)
    density = chain(jnp.stack([cos, energy, weight]), tab, w, True)[:, 0]
    density = lax.psum_scatter(density, "en", scatter_dimension=0, tiled=True)
    summed = lax.psum(density, "kt")
    potential_out = jnp.dot(summed - doping, poisson_inverse.T, precision=lax.Precision.HIGHEST)
    return summed, potential_out


def solution(mesh):
    return jax.shard_map(
        body,
        mesh=mesh,
        in_specs=(P("kt"), P(), P("en", None), P("en", None), P("en", None), P("en", None, None), P("en", None, None),
                  P("en", None), P()),
        out_specs=(P("en", None), P("en", None)),
        check_vma=False,
    )
```

```python
import jax
import jax.numpy as jnp
from jax import lax
from jax.experimental import pallas as pl
from jax.experimental.pallas import tpu as pltpu
from jax.sharding import PartitionSpec as P

f32, bf16 = jnp.float32, jnp.bfloat16
NT = (((1,), (1,)), ((), ()))
MESH = pl.DeviceIdType.MESH

BOTTOM, GAP, FILLING, SPREAD = -1.0, 0.25, -0.5, 0.1
BROADENING, CONTACT = 1.0, 0.5
NX, NY, NZ, EN, CORES = 4, 4, 4, 4, 2
LANES = 128
AHEAD_ROW, AHEAD_PLANE, AHEAD_CHIP = 5, 3, 1


def kernel(
    scal_ref, contact_ref, tab_in, base_ref, wave_ref, doping_ref, inverse_ref,
    den_out, pot_out,
    w_ref, tab_ref, g_ref, l_ref, c_ref, den_ref, sib_ref, chip_ref, line_in, line_ref, plane_in,
    load_sem, tab_sems, z_sems, row_sems, plane_sems, chip_sems, sib_sems, line_sems, last_sems,
):
    kt, e = lax.axis_index("kt"), lax.axis_index("en")
    x, y, zl, c = kt // 32, (kt // 8) % 4, (kt // 2) % 4, kt % 2
    z = e * NZ + zl
    slabs, n = base_ref.shape[0], base_ref.shape[-1]
    pairs = slabs * EN // CORES
    own_pairs = slabs // CORES
    blocks = n // LANES
    part = 2 * n // (NX * NY)

    def device(x, y, z, c):
        return (((x % NX) * NY + y % NY) * NZ + z % NZ) * CORES + c, (z // NZ) % EN

    def remote(src, dst, sems, index, where):
        return pltpu.make_async_remote_copy(
            src, dst, sems.at[(0, *index)], sems.at[(1, *index)], device_id=where, device_id_type=MESH
        )

    a, b = x + c * (y - x), y + c * (x - y)
    sibling = device(x, y, z, 1 - c)

    def step_row(d):
        return device(x + (1 - c) * d, y + c * d, z, c)

    def step_plane(d):
        return device(x + c * d, y + (1 - c) * d, z, c)

    def rows(first, count):
        return pl.ds(pl.multiple_of(first, 16), count)

    barrier = pltpu.get_barrier_semaphore()
    for d in range(1, NZ * EN):
        pl.semaphore_signal(barrier, 1, device_id=device(x, y, (z + d) % (NZ * EN), c), device_id_type=MESH)
    for d in range(1, NX * NY):
        pl.semaphore_signal(barrier, 1, device_id=device(x + d // NY, y + d % NY, z, c), device_id_type=MESH)
    pl.semaphore_signal(barrier, 1, device_id=sibling, device_id_type=MESH)

    def loads(i):
        s = e * slabs + i
        return (
            pltpu.make_async_copy(base_ref.at[i], w_ref.at[s, :n], load_sem.at[0, i]),
            pltpu.make_async_copy(wave_ref.at[i], w_ref.at[s, n:], load_sem.at[1, i]),
        )

    for i in range(slabs):
        for copy in loads(i):
            copy.start()
    tab_ref[e] = tab_in[...]
    pl.semaphore_wait(barrier, NZ * EN + NX * NY - 1)

    def send_tab(d):
        return remote(tab_in, tab_ref.at[e], tab_sems, (d - 1,), (kt, (e + d) % EN))

    def send_z(i, d):
        k = e * own_pairs + i
        piece = rows(part * (4 * b + a), part)
        here = w_ref.at[2 * k + c, piece]
        return remote(here, here, z_sems, (i, d - 1), (kt, (e + d) % EN))

    def wait_z(k):
        piece = w_ref.at[2 * k + c, rows(part * (4 * b + a), part)]
        d = (e - k // own_pairs + EN) % EN
        remote(piece, piece, z_sems, (k % own_pairs, d - 1), sibling).wait_recv()

    def send_row(k, d):
        here = w_ref.at[2 * k + c, rows(part * (4 * b + a), part)]
        return remote(here, here, row_sems, (k, d - 1), step_row(d))

    def send_plane(k, d):
        here = w_ref.at[2 * k + c, rows(part * 4 * b, 4 * part)]
        return remote(here, here, plane_sems, (k, d - 1), step_plane(d))

    def send_chip(k):
        here = w_ref.at[2 * k + c]
        return remote(here, here, chip_sems, (k,), sibling)

    def foreign(k):
        return jnp.logical_and(jnp.logical_and(k >= 0, k < pairs), k // own_pairs != e)

    def advance(k):
        at_row, at_plane, at_chip = k + AHEAD_ROW, k + AHEAD_PLANE, k + AHEAD_CHIP

        @pl.when(foreign(at_row))
        def _():
            wait_z(at_row)
            for d in range(1, 4):
                send_row(at_row, d).start()

        @pl.when(foreign(at_plane))
        def _():
            for d in range(1, 4):
                send_row(at_plane, d).wait_recv()
            for d in range(1, 4):
                send_plane(at_plane, d).start()

        @pl.when(foreign(at_chip))
        def _():
            for d in range(1, 4):
                send_plane(at_chip, d).wait_recv()
            send_chip(at_chip).start()

    for d in range(1, EN):
        send_tab(d).start()
    for i in range(slabs):
        for copy in loads(i):
            copy.wait()
    for i in range(own_pairs):
        for d in range(1, EN):
            send_z(i, d).start()

    def prologue(k, carry):
        advance(k)
        return carry

    lax.fori_loop(-AHEAD_ROW, 0, prologue, 0)
    for d in range(1, EN):
        send_tab(d).wait_recv()

    cos, energy, weight = scal_ref[0], scal_ref[1], scal_ref[2]
    eye = lax.broadcasted_iota(jnp.int32, (LANES, LANES), 0) == lax.broadcasted_iota(jnp.int32, (LANES, LANES), 1)

    def inverse_diag(s):
        group, local = s // slabs, s % slabs
        touches = jnp.logical_or(contact_ref[0] == s, contact_ref[1] == s)
        di = BROADENING + CONTACT * touches.astype(f32)
        dr = energy + tab_ref[group, pl.ds(local, 1), :] - cos * tab_ref[group, pl.ds(slabs + local, 1), :]
        mag = dr * dr + di * di
        return dr / mag, -di / mag

    def put_density(s, j, value):
        den_ref[s // slabs, pl.ds(slabs * j + s % slabs, 1), :] = value

    den_ref[...] = jnp.zeros_like(den_ref)
    g_ref[...] = jnp.zeros_like(g_ref)
    br, bi = inverse_diag(0)
    for i in range(blocks):
        sl = slice(LANES * i, LANES * (i + 1))
        g_ref[2 * LANES * i:2 * LANES * i + LANES, sl] = jnp.where(eye, br[:, sl], 0.0).astype(bf16)
        g_ref[2 * LANES * i + LANES:2 * LANES * (i + 1), sl] = jnp.where(eye, bi[:, sl], 0.0).astype(bf16)
        put_density(0, i, -weight * bi[:, sl])

    def slab(s):
        br, bi = inverse_diag(s)
        brc = jnp.transpose(jnp.broadcast_to(br, (LANES, n)))
        bic = jnp.transpose(jnp.broadcast_to(bi, (LANES, n)))
        c_ref[...] = (w_ref[s, :n].astype(f32) + cos * w_ref[s, n:].astype(f32)).astype(bf16)
        for j in range(blocks):
            left = lax.dot_general(
                c_ref[...], g_ref[2 * LANES * j:2 * LANES * (j + 1), :], NT, preferred_element_type=f32
            ).astype(bf16)
            sl = slice(LANES * j, LANES * (j + 1))
            for i in range(blocks):
                piece = left[LANES * i:LANES * (i + 1)]
                l_ref[2 * LANES * i:2 * LANES * i + LANES, sl] = piece[:, :LANES]
                l_ref[2 * LANES * i + LANES:2 * LANES * (i + 1), sl] = piece[:, LANES:]
        for j in range(blocks):
            lo = LANES * j
            sl = slice(lo, lo + LANES)
            energy_part = lax.dot_general(
                c_ref[lo:, :], l_ref[2 * lo:2 * lo + 2 * LANES, :], NT, preferred_element_type=f32
            )
            for i in range(j, blocks):
                piece = energy_part[LANES * i - lo:LANES * (i + 1) - lo]
                se_r, se_i = piece[:, :LANES], piece[:, LANES:]
                cr, ci = brc[LANES * i:LANES * (i + 1)], bic[LANES * i:LANES * (i + 1)]
                rr, ri = br[:, sl], bi[:, sl]
                hr = cr * se_r - ci * se_i
                hi = cr * se_i + ci * se_r
                gr = hr * rr - hi * ri
                gi = hr * ri + hi * rr
                if i == j:
                    gr = gr + jnp.where(eye, rr, 0.0)
                    gi = gi + jnp.where(eye, ri, 0.0)
                    put_density(s, j, -weight * jnp.sum(jnp.where(eye, gi, 0.0), axis=0, keepdims=True))
                gr, gi = gr.astype(bf16), gi.astype(bf16)
                g_ref[2 * LANES * i:2 * LANES * i + LANES, sl] = gr
                g_ref[2 * LANES * i + LANES:2 * LANES * (i + 1), sl] = gi
                if i > j:
                    si = slice(LANES * i, LANES * (i + 1))
                    g_ref[2 * lo:2 * lo + LANES, si] = jnp.transpose(gr)
                    g_ref[2 * lo + LANES:2 * lo + 2 * LANES, si] = jnp.transpose(gi)

    def chain(s, carry):
        k = s // CORES

        @pl.when(s % CORES == 0)
        def _():
            advance(k)

            @pl.when(foreign(k))
            def _():
                there = w_ref.at[2 * k + 1 - c]
                remote(there, there, chip_sems, (k,), sibling).wait_recv()

        @pl.when(s > 0)
        def _():
            slab(s)

        return carry

    lax.fori_loop(0, slabs * EN, chain, 0)

    both = remote(den_ref, sib_ref, sib_sems, (), sibling)
    both.start()
    both.wait_recv()
    chip_ref[...] = den_ref[...] + sib_ref[...]

    def send_line(d):
        to = (z + d) % (NZ * EN)
        return remote(chip_ref.at[to // NZ], line_in.at[z], line_sems, (d - 1,), device(x, y, to, c))

    for d in range(1, NZ * EN):
        send_line(d).start()
    line_in[z] = chip_ref[e]
    for d in range(1, NZ * EN):
        remote(chip_ref.at[e], line_in.at[(z + NZ * EN - d) % (NZ * EN)], line_sems, (d - 1,), sibling).wait_recv()
    line = line_in[0]
    for i in range(1, NZ * EN):
        line = line + line_in[i]
    line_ref[...] = line

    def send_last(d):
        return remote(
            line_ref, plane_in.at[x * NY + y], last_sems, (d - 1,), device(x + d // NY, y + d % NY, z, c)
        )

    for d in range(1, NX * NY):
        send_last(d).start()
    plane_in[x * NY + y] = line
    for d in range(1, NX * NY):
        sender = ((x - d // NY + NX) % NX) * NY + (y - d % NY + NY) % NY
        remote(line_ref, plane_in.at[sender], last_sems, (d - 1,), sibling).wait_recv()
    total = plane_in[0]
    for i in range(1, NX * NY):
        total = total + plane_in[i]
    pot = jnp.zeros((slabs, n), f32)
    for j in range(blocks):
        sl = slice(LANES * j, LANES * (j + 1))
        block = total[slabs * j:slabs * (j + 1), :]
        den_out[:, sl] = block
        pot = pot + lax.dot_general(
            block - doping_ref[:, sl], inverse_ref[:, sl], NT,
            precision=lax.Precision.HIGHEST, preferred_element_type=f32,
        )
    pot_out[...] = pot

    for d in range(1, EN):
        send_tab(d).wait_send()
        for i in range(own_pairs):
            send_z(i, d).wait_send()

    def left(k, carry):
        @pl.when(foreign(k))
        def _():
            for d in range(1, 4):
                send_row(k, d).wait_send()
                send_plane(k, d).wait_send()
            send_chip(k).wait_send()

        return carry

    lax.fori_loop(0, pairs, left, 0)
    both.wait_send()
    for d in range(1, NZ * EN):
        send_line(d).wait_send()
    for d in range(1, NX * NY):
        send_last(d).wait_send()


def body(counts, contact_slabs, onsite, hopping, potential_in, couple_base, couple_wave, doping, poisson_inverse):
    kt_size = lax.axis_size("kt")
    q, e = lax.axis_index("kt"), lax.axis_index("en")
    slabs, n = onsite.shape
    cos = jnp.cos(jnp.pi * (q.astype(f32) + 0.5) / kt_size)
    energy = BOTTOM + GAP * e.astype(f32)
    weight = GAP / (1.0 + jnp.exp((energy - FILLING) / SPREAD)) / jnp.pi
    weight = jnp.where(e < counts[0], weight, 0.0)
    tab = jnp.concatenate([-onsite - potential_in, hopping], 0)
    total = slabs * EN
    pairs = total // CORES
    vmem, smem = pl.BlockSpec(memory_space=pltpu.VMEM), pl.BlockSpec(memory_space=pltpu.SMEM)
    anywhere = pl.BlockSpec(memory_space=pl.ANY)
    piece = (4 * slabs, LANES)
    sems = pltpu.SemaphoreType.DMA
    return pl.pallas_call(
        kernel,
        out_shape=(jax.ShapeDtypeStruct((slabs, n), f32), jax.ShapeDtypeStruct((slabs, n), f32)),
        in_specs=[smem, smem, vmem, anywhere, anywhere, vmem, vmem],
        out_specs=(vmem, vmem),
        scratch_shapes=[
            pltpu.VMEM((total, 2 * n, n), bf16),
            pltpu.VMEM((EN, 2 * slabs, n), f32),
            pltpu.VMEM((2 * n, n), bf16),
            pltpu.VMEM((2 * n, n), bf16),
            pltpu.VMEM((n, n), bf16),
            pltpu.VMEM((EN, *piece), f32),
            pltpu.VMEM((EN, *piece), f32),
            pltpu.VMEM((EN, *piece), f32),
            pltpu.VMEM((NZ * EN, *piece), f32),
            pltpu.VMEM(piece, f32),
            pltpu.VMEM((NX * NY, *piece), f32),
            sems((2, slabs)),
            sems((2, EN - 1)),
            sems((2, slabs // CORES, EN - 1)),
            sems((2, pairs, 3)),
            sems((2, pairs, 3)),
            sems((2, pairs)),
            sems((2,)),
            sems((2, NZ * EN - 1)),
            sems((2, NX * NY - 1)),
        ],
        compiler_params=pltpu.CompilerParams(collective_id=0, has_side_effects=True, vmem_limit_bytes=40 * 2**20),
    )(jnp.stack([cos, energy, weight]), contact_slabs, tab, couple_base, couple_wave, doping, poisson_inverse)


def solution(mesh):
    return jax.shard_map(
        body,
        mesh=mesh,
        in_specs=(
            P("kt"), P(), P("en", None), P("en", None), P("en", None),
            P("en", None, None), P("en", None, None), P("en", None), P(),
        ),
        out_specs=(P("en", None), P("en", None)),
        check_vma=False,
    )
```

```python
import jax
import jax.numpy as jnp
from jax import lax
from jax.experimental import pallas as pl
from jax.experimental.pallas import tpu as pltpu
from jax.sharding import PartitionSpec as P

f32, bf16 = jnp.float32, jnp.bfloat16
NT = (((1,), (1,)), ((), ()))
MESH = pl.DeviceIdType.MESH

BOTTOM, GAP, FILLING, SPREAD = -1.0, 0.25, -0.5, 0.1
BROADENING, CONTACT = 1.0, 0.5
NX, NY, NZ, EN, CORES = 4, 4, 4, 4, 2
PLANE = NX * NY
LANES, SUB = 128, 8
SOURCES = ((4, (3, 2, 1, 0)), (8, (3, 2)), (11, (0, 1)), (15, (0, 1, 2, 3)))


def kernel(
    counts_in, contact_in, onsite_in, hopping_in, potential_in, base_ref, wave_ref, doping_in, inverse_in,
    den_out, pot_out,
    w_ref, tab_ref, tab_own, rows_ref, doping_ref, inverse_ref, counts_ref, contact_ref,
    count_in, count_mine, count_all, par_ref, g_ref, l_ref, c_ref, den_ref, plane_in, sum_ref, last_in,
    load_sems, small_sems, tab_sems, count_sems, zone_sems, z_send, z_recv, row_sems, plane_sems, chip_sems,
    sum_sems, last_send, last_recv, ready_sem,
):
    kt, e = lax.axis_index("kt"), lax.axis_index("en")
    x, y, zl, c = kt // 32, (kt // 8) % 4, (kt // 2) % 4, kt % 2
    xy = x * NY + y
    slabs, n = base_ref.shape[0], base_ref.shape[-1]
    total = slabs * EN
    pairs, own_pairs = total // CORES, slabs // CORES
    blocks = n // LANES
    part = 2 * n // PLANE

    def place(x, y, zl, c):
        return (((x % NX) * NY + y % NY) * NZ + zl % NZ) * CORES + c % CORES

    def remote(src, dst, send, recv, where):
        return pltpu.make_async_remote_copy(src, dst, send, recv, device_id=where, device_id_type=MESH)

    def rows(first, count):
        return pl.ds(pl.multiple_of(first, 16), count)

    a, b = x + c * (y - x), y + c * (x - y)
    piece_at = 4 * b + a
    barrier = pltpu.get_barrier_semaphore()

    def in_plane(d):
        return place(x + d // NY, y + d % NY, zl, c), e

    def zone(d):
        return place(x, y, zl + d // CORES, c + d % CORES), e

    small = [
        pltpu.make_async_copy(src, dst, small_sems.at[i])
        for i, (src, dst) in enumerate((
            (onsite_in, rows_ref.at[0]), (potential_in, rows_ref.at[1]), (hopping_in, rows_ref.at[2]),
            (doping_in, doping_ref), (inverse_in, inverse_ref), (counts_in, counts_ref), (contact_in, contact_ref),
        ))
    ]
    for copy in small:
        copy.start()

    def send_last(group, d):
        return remote(
            sum_ref.at[group], last_in.at[zl * CORES + c], last_send.at[group, d], last_recv.at[zl * CORES + c],
            (place(x, y, d // CORES, d % CORES), group),
        )

    def finish():
        acc = last_in[0]
        for i in range(1, NZ * CORES):
            acc = acc + last_in[i]
        pot = jnp.zeros((slabs, n), f32)
        for j in range(blocks):
            sl = slice(LANES * j, LANES * (j + 1))
            block = acc[slabs * j:slabs * (j + 1), :]
            den_out[:, sl] = block
            pot = pot + lax.dot_general(
                block - doping_ref[:, sl], inverse_ref[:, sl], NT,
                precision=lax.Precision.HIGHEST, preferred_element_type=f32,
            )
        pot_out[...] = pot

    def make_tab():
        for copy in small[:3]:
            copy.wait()
        tab_own[:slabs] = -rows_ref[0] - rows_ref[1]
        tab_own[slabs:] = rows_ref[2]

    def tab_copy(run):
        return remote(tab_own, tab_ref.at[run], tab_sems.at[0], tab_sems.at[run], (kt, 0))

    @pl.when(e != 0)
    def _():
        make_tab()
        pl.semaphore_wait(barrier, NZ * CORES)
        for d in range(NZ * CORES):
            pl.semaphore_signal(
                ready_sem, 1, device_id=(place(x, y, d // CORES, d % CORES), 0), device_id_type=MESH
            )

        def send_z(source, first, i, slot, to):
            run = source // NZ
            k = run * own_pairs + i
            local = 2 * i + c
            ref = base_ref if first else wave_ref
            index = piece_at if first else piece_at - PLANE // 2
            return remote(
                ref.at[local, rows(part * index, part)],
                w_ref.at[2 * k + c, rows(part * piece_at, part)],
                z_send.at[i, slot], z_recv.at[k], (place(x, y, to, c), 0),
            )

        for act in ("start", "wait_send"):
            for source, targets in SOURCES:
                for first in (True, False):
                    in_half = (piece_at < PLANE // 2) if first else (piece_at >= PLANE // 2)

                    @pl.when(jnp.logical_and(e * NZ + zl == source, in_half))
                    def _():
                        for i in range(own_pairs):
                            for slot, to in enumerate(targets):
                                getattr(send_z(source, first, i, slot, to), act)()

            if act == "start":
                tab_copy(e).start()
        tab_copy(e).wait_send()
        for i in range(NZ * CORES):
            remote(sum_ref.at[0], last_in.at[i], last_send.at[0, 0], last_recv.at[i], (kt, 0)).wait_recv()
        for copy in small[3:]:
            copy.wait()
        finish()

    @pl.when(e == 0)
    def _():
        def loads(i):
            return (
                pltpu.make_async_copy(base_ref.at[i], w_ref.at[i, :n], load_sems.at[0, i]),
                pltpu.make_async_copy(wave_ref.at[i], w_ref.at[i, n:], load_sems.at[1, i]),
            )

        for i in range(1, slabs):
            for copy in loads(i):
                copy.start()
        for d in range(1, PLANE):
            pl.semaphore_signal(barrier, 1, device_id=in_plane(d), device_id_type=MESH)
        for d in range(1, NZ * CORES):
            pl.semaphore_signal(barrier, 1, device_id=zone(d), device_id_type=MESH)
        for run in range(1, EN):
            for d in range(NZ * CORES):
                pl.semaphore_signal(
                    barrier, 1, device_id=(place(x, y, d // CORES, d % CORES), run), device_id_type=MESH
                )

        lane = lax.broadcasted_iota(jnp.int32, (SUB, LANES), 1)
        momentum = (lane % PLANE) * (NZ * CORES) + lane // PLANE
        cosines = jnp.cos(jnp.pi * (momentum.astype(f32) + 0.5) / (PLANE * NZ * CORES))
        me = (zl * CORES + c) * PLANE + xy

        def set_params(item, cosine, j):
            energy = BOTTOM + GAP * j
            par_ref[item, 0] = cosine
            par_ref[item, 1] = energy
            par_ref[item, 2] = GAP / (1.0 + jnp.exp((energy - FILLING) / SPREAD)) / jnp.pi

        def pick(mask, values):
            return jnp.broadcast_to(jnp.sum(jnp.where(mask, values, 0.0), axis=1, keepdims=True), (SUB, LANES))

        set_params(0, pick(lane == me, cosines), jnp.zeros((SUB, LANES), f32))
        make_tab()
        tab_ref[0] = tab_own[...]
        for copy in small[5:]:
            copy.wait()
        den_ref[...] = jnp.zeros_like(den_ref)

        eye = lax.broadcasted_iota(jnp.int32, (LANES, LANES), 0) == lax.broadcasted_iota(jnp.int32, (LANES, LANES), 1)

        def wide(item, which):
            row = par_ref[item, which, 0:1, :]
            return jnp.concatenate([row] * blocks, axis=1)

        def inverse_diag(item, s):
            group, local = s // slabs, s % slabs
            touches = jnp.logical_or(contact_ref[0] == s, contact_ref[1] == s)
            di = BROADENING + CONTACT * touches.astype(f32)
            dr = (
                wide(item, 1) + tab_ref[group, pl.ds(local, 1), :]
                - wide(item, 0) * tab_ref[group, pl.ds(slabs + local, 1), :]
            )
            mag = dr * dr + di * di
            return dr / mag, -di / mag

        def add_density(s, j, value):
            at = pl.ds(slabs * j + s % slabs, 1)
            den_ref[s // slabs, at, :] = den_ref[s // slabs, at, :] + value

        def first_slab(item):
            g = g_ref.at[item]
            g[...] = jnp.zeros_like(g)
            br, bi = inverse_diag(item, 0)
            for i in range(blocks):
                sl = slice(LANES * i, LANES * (i + 1))
                g[2 * LANES * i:2 * LANES * i + LANES, sl] = jnp.where(eye, br[:, sl], 0.0).astype(bf16)
                g[2 * LANES * i + LANES:2 * LANES * (i + 1), sl] = jnp.where(eye, bi[:, sl], 0.0).astype(bf16)
                add_density(0, i, -par_ref[item, 2, 0:1, :] * bi[:, sl])

        def couple(item, s):
            cosine = wide(item, 0)
            c_ref[item] = (w_ref[s, :n].astype(f32) + cosine * w_ref[s, n:].astype(f32)).astype(bf16)

        def left_product(item):
            for j in range(blocks):
                left = lax.dot_general(
                    c_ref[item], g_ref[item, 2 * LANES * j:2 * LANES * (j + 1), :], NT, preferred_element_type=f32
                ).astype(bf16)
                sl = slice(LANES * j, LANES * (j + 1))
                for i in range(blocks):
                    piece = left[LANES * i:LANES * (i + 1)]
                    l_ref[item, 2 * LANES * i:2 * LANES * i + LANES, sl] = piece[:, :LANES]
                    l_ref[item, 2 * LANES * i + LANES:2 * LANES * (i + 1), sl] = piece[:, LANES:]

        def green(item, s):
            br, bi = inverse_diag(item, s)
            brc = jnp.transpose(jnp.broadcast_to(br, (LANES, n)))
            bic = jnp.transpose(jnp.broadcast_to(bi, (LANES, n)))
            for j in range(blocks):
                lo = LANES * j
                sl = slice(lo, lo + LANES)
                energy_part = lax.dot_general(
                    c_ref[item, lo:, :], l_ref[item, 2 * lo:2 * lo + 2 * LANES, :], NT, preferred_element_type=f32
                )
                for i in range(j, blocks):
                    piece = energy_part[LANES * i - lo:LANES * (i + 1) - lo]
                    se_r, se_i = piece[:, :LANES], piece[:, LANES:]
                    cr, ci = brc[LANES * i:LANES * (i + 1)], bic[LANES * i:LANES * (i + 1)]
                    rr, ri = br[:, sl], bi[:, sl]
                    hr = cr * se_r - ci * se_i
                    hi = cr * se_i + ci * se_r
                    gr = hr * rr - hi * ri
                    gi = hr * ri + hi * rr
                    if i == j:
                        gr = gr + jnp.where(eye, rr, 0.0)
                        gi = gi + jnp.where(eye, ri, 0.0)
                        add_density(
                            s, j, -par_ref[item, 2, 0:1, :] * jnp.sum(jnp.where(eye, gi, 0.0), axis=0, keepdims=True)
                        )
                    gr, gi = gr.astype(bf16), gi.astype(bf16)
                    g_ref[item, 2 * LANES * i:2 * LANES * i + LANES, sl] = gr
                    g_ref[item, 2 * LANES * i + LANES:2 * LANES * (i + 1), sl] = gi
                    if i > j:
                        si = slice(LANES * i, LANES * (i + 1))
                        g_ref[item, 2 * lo:2 * lo + LANES, si] = jnp.transpose(gr)
                        g_ref[item, 2 * lo + LANES:2 * lo + 2 * LANES, si] = jnp.transpose(gi)

        def slab(items, s):
            for item in items:
                couple(item, s)
            for item in items:
                left_product(item)
            for item in items:
                green(item, s)

        def own_piece(k):
            return w_ref.at[2 * k + c, rows(part * piece_at, part)]

        def send_row(k, d):
            to = place(x + (1 - c) * d, y + c * d, zl, c), e
            return remote(own_piece(k), own_piece(k), row_sems.at[0, k, d - 1], row_sems.at[1, k, d - 1], to)

        def send_plane(k, d):
            here = w_ref.at[2 * k + c, rows(part * 4 * b, 4 * part)]
            to = place(x + c * d, y + (1 - c) * d, zl, c), e
            return remote(here, here, plane_sems.at[0, k, d - 1], plane_sems.at[1, k, d - 1], to)

        def send_chip(k):
            here = w_ref.at[2 * k + c]
            return remote(here, here, chip_sems.at[0, k], chip_sems.at[1, k], (place(x, y, zl, 1 - c), e))

        def stage_row(k):
            @pl.when(k < pairs)
            def _():
                remote(own_piece(k), own_piece(k), z_send.at[0, 0], z_recv.at[k], (kt, 1)).wait_recv()
                for d in range(1, 4):
                    send_row(k, d).start()

        def stage_plane(k):
            @pl.when(k < pairs)
            def _():
                for d in range(1, 4):
                    send_row(k, d).wait_recv()
                for d in range(1, 4):
                    send_plane(k, d).start()

        def stage_chip(k):
            @pl.when(k < pairs)
            def _():
                for d in range(1, 4):
                    send_plane(k, d).wait_recv()
                send_chip(k).start()

        def stage_here(k):
            there = w_ref.at[2 * k + 1 - c]
            remote(there, there, chip_sems.at[0, k], chip_sems.at[1, k], (place(x, y, zl, 1 - c), e)).wait_recv()

        def send_sum(group, d):
            return remote(
                den_ref.at[group], plane_in.at[group, xy], sum_sems.at[0, group, d - 1], sum_sems.at[1, group, d - 1],
                in_plane(d),
            )

        def start_sum(group):
            for d in range(1, PLANE):
                send_sum(group, d).start()
            plane_in[group, xy] = den_ref[group]

        def end_sum(group):
            for d in range(1, PLANE):
                sender = ((x - d // NY + NX) % NX) * NY + (y - d % NY + NY) % NY
                remote(
                    den_ref.at[group], plane_in.at[group, sender], sum_sems.at[0, group, d - 1],
                    sum_sems.at[1, group, d - 1], in_plane(d),
                ).wait_recv()
            acc = plane_in[group, 0]
            for i in range(1, PLANE):
                acc = acc + plane_in[group, i]
            sum_ref[group] = acc
            for d in range(NZ * CORES):
                if group == 0:
                    @pl.when(d != zl * CORES + c)
                    def _():
                        send_last(group, d).start()
                else:
                    send_last(group, d).start()

        first_slab(0)
        for i in range(1, slabs):
            for copy in loads(i):
                copy.wait()

        def alone(item):
            def step(s, carry):
                slab((item,), s)
                return carry

            return step

        lax.fori_loop(1, slabs, alone(0), 0)

        pl.semaphore_wait(barrier, PLANE - 1 + NZ * CORES - 1)
        mine = jnp.zeros((SUB, LANES), jnp.int32) + counts_ref[0]
        count_mine[0] = mine.astype(f32)

        def send_count(d):
            return remote(
                count_mine.at[0], count_in.at[xy], count_sems.at[0, d - 1], count_sems.at[1, d - 1], in_plane(d)
            )

        for d in range(1, PLANE):
            send_count(d).start()
        count_in[xy] = count_mine[0]
        for d in range(1, PLANE):
            sender = ((x - d // NY + NX) % NX) * NY + (y - d % NY + NY) % NY
            remote(
                count_mine.at[0], count_in.at[sender], count_sems.at[0, d - 1], count_sems.at[1, d - 1], in_plane(d)
            ).wait_recv()
        here = (zl * CORES + c) * PLANE
        line = jnp.zeros((SUB, LANES), f32)
        for i in range(PLANE):
            line = line + jnp.where(lane == here + i, count_in[i], 0.0)
        count_mine[1] = line

        def send_zone(d):
            return remote(
                count_mine.at[1], count_all.at[zl * CORES + c], zone_sems.at[0, d - 1], zone_sems.at[1, d - 1], zone(d)
            )

        for d in range(1, NZ * CORES):
            send_zone(d).start()
        count_all[zl * CORES + c] = line
        stage_row(own_pairs)
        stage_row(own_pairs + 1)
        stage_plane(own_pairs)
        for d in range(1, NZ * CORES):
            from_z, from_c = (zl - d // CORES + NZ) % NZ, (c + d) % CORES
            remote(
                count_mine.at[1], count_all.at[from_z * CORES + from_c], zone_sems.at[0, d - 1],
                zone_sems.at[1, d - 1], zone(d),
            ).wait_recv()
        every = count_all[0]
        for i in range(1, NZ * CORES):
            every = every + count_all[i]
        extra = every - 1.0
        upper = (
            lax.broadcasted_iota(jnp.int32, (LANES, LANES), 0) <= lax.broadcasted_iota(jnp.int32, (LANES, LANES), 1)
        )
        upto = jnp.dot(extra.astype(bf16), upper.astype(f32).astype(bf16), preferred_element_type=f32)
        before = upto - extra
        mine_f = jnp.zeros((SUB, LANES), jnp.int32) + me
        mine_f = mine_f.astype(f32)
        owner = jnp.logical_and(before <= mine_f, mine_f < upto)
        set_params(1, pick(owner, cosines), pick(owner, 1.0 + mine_f - before))
        first_slab(1)
        stage_row(own_pairs + 2)
        stage_plane(own_pairs + 1)
        slab((1,), 1)
        stage_chip(own_pairs)
        slab((1,), 2)
        stage_row(own_pairs + 3)
        stage_plane(own_pairs + 2)
        slab((1,), 3)
        start_sum(0)
        for run in range(1, EN):
            remote(tab_own, tab_ref.at[run], tab_sems.at[0], tab_sems.at[run], (kt, 0)).wait_recv()

        def both(s, carry):
            k = s // CORES

            @pl.when(s % CORES == 0)
            def _():
                stage_chip(k + 1)
                stage_here(k)

            @pl.when(s % CORES == 1)
            def _():
                stage_row(k + 4)
                stage_plane(k + 3)

            slab((0, 1), s)
            return carry

        lax.fori_loop(slabs, 2 * slabs, both, 0)
        start_sum(1)
        pl.semaphore_wait(ready_sem, (EN - 1) * NZ * CORES)
        end_sum(0)
        lax.fori_loop(2 * slabs, 3 * slabs, both, 0)
        start_sum(2)
        end_sum(1)
        lax.fori_loop(3 * slabs, 4 * slabs, both, 0)
        start_sum(3)
        end_sum(2)
        end_sum(3)

        last_in[zl * CORES + c] = sum_ref[0]
        for d in range(1, NZ * CORES):
            at = (zl * CORES + c + d) % (NZ * CORES)
            remote(sum_ref.at[0], last_in.at[at], last_send.at[0, 0], last_recv.at[at], (kt, 1)).wait_recv()
        for copy in small[3:5]:
            copy.wait()
        finish()

        for d in range(1, PLANE):
            send_count(d).wait_send()
        for d in range(1, NZ * CORES):
            send_zone(d).wait_send()

        def left(k, carry):
            for d in range(1, 4):
                send_row(k, d).wait_send()
                send_plane(k, d).wait_send()
            send_chip(k).wait_send()
            return carry

        lax.fori_loop(own_pairs, pairs, left, 0)
        for group in range(EN):
            for d in range(1, PLANE):
                send_sum(group, d).wait_send()
            for d in range(NZ * CORES):
                if group == 0:
                    @pl.when(d != zl * CORES + c)
                    def _():
                        send_last(group, d).wait_send()
                else:
                    send_last(group, d).wait_send()


def body(counts, contact_slabs, onsite, hopping, potential_in, couple_base, couple_wave, doping, poisson_inverse):
    slabs, n = onsite.shape
    total = slabs * EN
    pairs = total // CORES
    vmem, anywhere = pl.BlockSpec(memory_space=pltpu.VMEM), pl.BlockSpec(memory_space=pl.ANY)
    piece = (4 * slabs, LANES)
    tile = (SUB, LANES)
    sems = pltpu.SemaphoreType.DMA
    return pl.pallas_call(
        kernel,
        out_shape=(jax.ShapeDtypeStruct((slabs, n), f32), jax.ShapeDtypeStruct((slabs, n), f32)),
        in_specs=[anywhere] * 9,
        out_specs=(vmem, vmem),
        scratch_shapes=[
            pltpu.VMEM((total, 2 * n, n), bf16),
            pltpu.VMEM((EN, 2 * slabs, n), f32),
            pltpu.VMEM((2 * slabs, n), f32),
            pltpu.VMEM((3, slabs, n), f32),
            pltpu.VMEM((slabs, n), f32),
            pltpu.VMEM((n, n), f32),
            pltpu.SMEM((1,), jnp.int32),
            pltpu.SMEM((2,), jnp.int32),
            pltpu.VMEM((PLANE, *tile), f32),
            pltpu.VMEM((2, *tile), f32),
            pltpu.VMEM((NZ * CORES, *tile), f32),
            pltpu.VMEM((2, 3, *tile), f32),
            pltpu.VMEM((2, 2 * n, n), bf16),
            pltpu.VMEM((2, 2 * n, n), bf16),
            pltpu.VMEM((2, n, n), bf16),
            pltpu.VMEM((EN, *piece), f32),
            pltpu.VMEM((EN, PLANE, *piece), f32),
            pltpu.VMEM((EN, *piece), f32),
            pltpu.VMEM((NZ * CORES, *piece), f32),
            sems((2, slabs)),
            sems((7,)),
            sems((EN,)),
            sems((2, PLANE - 1)),
            sems((2, NZ * CORES - 1)),
            sems((slabs // CORES, NZ)),
            sems((pairs,)),
            sems((2, pairs, 3)),
            sems((2, pairs, 3)),
            sems((2, pairs)),
            sems((2, EN, PLANE - 1)),
            sems((EN, NZ * CORES)),
            sems((NZ * CORES,)),
            pltpu.SemaphoreType.REGULAR,
        ],
        compiler_params=pltpu.CompilerParams(collective_id=0, has_side_effects=True, vmem_limit_bytes=40 * 2**20),
    )(counts, contact_slabs, onsite, hopping, potential_in, couple_base, couple_wave, doping, poisson_inverse)


def solution(mesh):
    return jax.shard_map(
        body,
        mesh=mesh,
        in_specs=(
            P("kt"), P(), P("en", None), P("en", None), P("en", None),
            P("en", None, None), P("en", None, None), P("en", None), P(),
        ),
        out_specs=(P("en", None), P("en", None)),
        check_vma=False,
    )
```

```python
import jax
import jax.numpy as jnp
from jax import lax
from jax.experimental import pallas as pl
from jax.experimental.pallas import tpu as pltpu
from jax.sharding import PartitionSpec as P

f32, bf16 = jnp.float32, jnp.bfloat16
NT = (((1,), (1,)), ((), ()))
NN = (((1,), (0,)), ((), ()))
MESH = pl.DeviceIdType.MESH

BOTTOM, GAP, FILLING, SPREAD = -1.0, 0.25, -0.5, 0.1
BROADENING, CONTACT = 1.0, 0.5
NX, NY, NZ, EN, CORES = 4, 4, 4, 4, 2
PLANE = NX * NY
LANES, SUB = 128, 8
SOURCES = ((4, (3, 2, 1, 0)), (8, (3, 2)), (11, (0, 1)), (15, (0, 1, 2, 3)))


def kernel(
    counts_in, contact_in, onsite_in, hopping_in, potential_in, base_ref, wave_ref, doping_in, inverse_in,
    den_out, pot_out,
    w_ref, tab_ref, tab_own, rows_ref, doping_ref, inverse_ref, counts_ref, contact_ref,
    count_in, count_mine, count_all, par_ref, g_ref, l_ref, c_ref, den_ref, line_in, line_ref, plane_in,
    load_sems, small_sems, tab_sems, count_sems, zone_sems, z_send, z_recv, row_sems, plane_sems, chip_sems,
    line_send, line_recv, sum_sems, ready_sem,
):
    kt, e = lax.axis_index("kt"), lax.axis_index("en")
    x, y, zl, c = kt // 32, (kt // 8) % 4, (kt // 2) % 4, kt % 2
    xy = x * NY + y
    slabs, n = base_ref.shape[0], base_ref.shape[-1]
    total = slabs * EN
    pairs, own_pairs = total // CORES, slabs // CORES
    blocks = n // LANES
    part = 2 * n // PLANE

    def place(x, y, zl, c):
        return (((x % NX) * NY + y % NY) * NZ + zl % NZ) * CORES + c % CORES

    def remote(src, dst, send, recv, where):
        return pltpu.make_async_remote_copy(src, dst, send, recv, device_id=where, device_id_type=MESH)

    def rows(first, count):
        return pl.ds(pl.multiple_of(first, 16), count)

    a, b = x + c * (y - x), y + c * (x - y)
    piece_at = 4 * b + a
    barrier = pltpu.get_barrier_semaphore()

    def in_plane(d):
        return place(x + d // NY, y + d % NY, zl, c), e

    def zone(d):
        return place(x, y, zl + d // CORES, c + d % CORES), e

    small = [
        pltpu.make_async_copy(src, dst, small_sems.at[i])
        for i, (src, dst) in enumerate((
            (onsite_in, rows_ref.at[0]), (potential_in, rows_ref.at[1]), (hopping_in, rows_ref.at[2]),
            (doping_in, doping_ref), (inverse_in, inverse_ref), (counts_in, counts_ref), (contact_in, contact_ref),
        ))
    ]
    for copy in small:
        copy.start()

    spot = zl * CORES + c

    def signal_plane():
        for d in range(1, PLANE):
            pl.semaphore_signal(barrier, 1, device_id=in_plane(d), device_id_type=MESH)

    def send_plane_sum(d):
        return remote(line_ref, plane_in.at[xy], sum_sems.at[0, d - 1], sum_sems.at[1, d - 1], in_plane(d))

    def sum_line(first):
        for d in range(first, NZ * CORES):
            at = (spot + d) % (NZ * CORES)
            remote(line_ref, line_in.at[at], line_send.at[0, 0], line_recv.at[at], (kt, 0)).wait_recv()
        acc = line_in[0]
        for i in range(1, NZ * CORES):
            acc = acc + line_in[i]
        line_ref[...] = acc
        plane_in[xy] = acc
        for d in range(1, PLANE):
            send_plane_sum(d).start()

    def finish():
        for copy in small[3:5]:
            copy.wait()
        for d in range(1, PLANE):
            sender = ((x - d // NY + NX) % NX) * NY + (y - d % NY + NY) % NY
            remote(line_ref, plane_in.at[sender], sum_sems.at[0, d - 1], sum_sems.at[1, d - 1], in_plane(d)).wait_recv()
        acc = plane_in[0]
        for i in range(1, PLANE):
            acc = acc + plane_in[i]
        pot = jnp.zeros((slabs, n), f32)
        for j in range(blocks):
            sl = slice(LANES * j, LANES * (j + 1))
            block = jnp.concatenate(
                [acc[i // CORES, blocks * (i % CORES) + j:blocks * (i % CORES) + j + 1] for i in range(slabs)], axis=0
            )
            den_out[:, sl] = block
            pot = pot + lax.dot_general(
                block - doping_ref[:, sl], inverse_ref[:, sl], NT,
                precision=lax.Precision.HIGHEST, preferred_element_type=f32,
            )
        pot_out[...] = pot
        for d in range(1, PLANE):
            send_plane_sum(d).wait_send()

    def make_tab():
        for copy in small[:3]:
            copy.wait()
        tab_own[:slabs] = -rows_ref[0] - rows_ref[1]
        tab_own[slabs:] = rows_ref[2]

    def tab_copy(run):
        return remote(tab_own, tab_ref.at[run], tab_sems.at[0], tab_sems.at[run], (kt, 0))

    @pl.when(e != 0)
    def _():
        signal_plane()
        pl.semaphore_wait(barrier, NZ * CORES + PLANE - 1)

        def send_z(source, first, i, slot, to):
            run = source // NZ
            k = run * own_pairs + i
            local = 2 * i + c
            ref = base_ref if first else wave_ref
            index = piece_at if first else piece_at - PLANE // 2
            return remote(
                ref.at[local, rows(part * index, part)],
                w_ref.at[2 * k + c, rows(part * piece_at, part)],
                z_send.at[i, slot], z_recv.at[k], (place(x, y, to, c), 0),
            )

        for act in ("start", "wait_send"):
            for source, targets in SOURCES:
                for first in (True, False):
                    in_half = (piece_at < PLANE // 2) if first else (piece_at >= PLANE // 2)

                    @pl.when(jnp.logical_and(e * NZ + zl == source, in_half))
                    def _():
                        for i in range(own_pairs):
                            for slot, to in enumerate(targets):
                                getattr(send_z(source, first, i, slot, to), act)()

            if act == "start":
                make_tab()
                tab_copy(e).start()
                for d in range(NZ * CORES):
                    pl.semaphore_signal(
                        ready_sem, 1, device_id=(place(x, y, d // CORES, d % CORES), 0), device_id_type=MESH
                    )
        tab_copy(e).wait_send()
        for copy in small[5:]:
            copy.wait()
        sum_line(0)
        finish()

    @pl.when(e == 0)
    def _():
        def loads(i):
            return (
                pltpu.make_async_copy(base_ref.at[i], w_ref.at[i, :n], load_sems.at[0, i]),
                pltpu.make_async_copy(wave_ref.at[i], w_ref.at[i, n:], load_sems.at[1, i]),
            )

        for i in range(1, slabs):
            for copy in loads(i):
                copy.start()
        signal_plane()
        for d in range(1, NZ * CORES):
            pl.semaphore_signal(barrier, 1, device_id=zone(d), device_id_type=MESH)
        for run in range(1, EN):
            for d in range(NZ * CORES):
                pl.semaphore_signal(
                    barrier, 1, device_id=(place(x, y, d // CORES, d % CORES), run), device_id_type=MESH
                )

        lane = lax.broadcasted_iota(jnp.int32, (SUB, LANES), 1)
        momentum = (lane % PLANE) * (NZ * CORES) + lane // PLANE
        cosines = jnp.cos(jnp.pi * (momentum.astype(f32) + 0.5) / (PLANE * NZ * CORES))
        me = (zl * CORES + c) * PLANE + xy

        def set_params(item, cosine, j):
            energy = BOTTOM + GAP * j
            par_ref[item, 0] = cosine
            par_ref[item, 1] = energy
            par_ref[item, 2] = GAP / (1.0 + jnp.exp((energy - FILLING) / SPREAD)) / jnp.pi

        def pick(mask, values):
            return jnp.broadcast_to(jnp.sum(jnp.where(mask, values, 0.0), axis=1, keepdims=True), (SUB, LANES))

        set_params(0, pick(lane == me, cosines), jnp.zeros((SUB, LANES), f32))
        make_tab()
        tab_ref[0] = tab_own[...]
        for copy in small[5:]:
            copy.wait()
        den_ref[...] = jnp.zeros_like(den_ref)

        eye = lax.broadcasted_iota(jnp.int32, (LANES, LANES), 0) == lax.broadcasted_iota(jnp.int32, (LANES, LANES), 1)

        def wide(item, which):
            row = par_ref[item, which, 0:1, :]
            return jnp.concatenate([row] * blocks, axis=1)

        def inverse_diag(item, s):
            group, local = s // slabs, s % slabs
            touches = jnp.logical_or(contact_ref[0] == s, contact_ref[1] == s)
            di = BROADENING + CONTACT * touches.astype(f32)
            dr = (
                wide(item, 1) + tab_ref[group, pl.ds(local, 1), :]
                - wide(item, 0) * tab_ref[group, pl.ds(slabs + local, 1), :]
            )
            mag = dr * dr + di * di
            return dr / mag, -di / mag

        def add_density(s, j, value):
            at = pl.ds(blocks * (s % CORES) + j, 1)
            den_ref[s // CORES, at, :] = den_ref[s // CORES, at, :] + value

        def first_slab(item):
            g = g_ref.at[item]
            g[...] = jnp.zeros_like(g)
            br, bi = inverse_diag(item, 0)
            for i in range(blocks):
                sl = slice(LANES * i, LANES * (i + 1))
                g[sl, 2 * LANES * i:2 * LANES * i + LANES] = jnp.where(eye, br[:, sl], 0.0).astype(bf16)
                g[sl, 2 * LANES * i + LANES:2 * LANES * (i + 1)] = jnp.where(eye, bi[:, sl], 0.0).astype(bf16)
                add_density(0, i, -par_ref[item, 2, 0:1, :] * bi[:, sl])

        def couple(item, s):
            cosine = wide(item, 0)
            c_ref[item] = (w_ref[s, :n].astype(f32) + cosine * w_ref[s, n:].astype(f32)).astype(bf16)

        def left_product(item):
            for j in range(blocks):
                left = lax.dot_general(
                    c_ref[item], g_ref[item, :, 2 * LANES * j:2 * LANES * (j + 1)], NN, preferred_element_type=f32
                ).astype(bf16)
                sl = slice(LANES * j, LANES * (j + 1))
                for i in range(blocks):
                    piece = left[LANES * i:LANES * (i + 1)]
                    l_ref[item, 2 * LANES * i:2 * LANES * i + LANES, sl] = piece[:, :LANES]
                    l_ref[item, 2 * LANES * i + LANES:2 * LANES * (i + 1), sl] = piece[:, LANES:]

        def green(item, s):
            br, bi = inverse_diag(item, s)
            brc = jnp.transpose(jnp.broadcast_to(br, (LANES, n)))
            bic = jnp.transpose(jnp.broadcast_to(bi, (LANES, n)))
            for j in range(blocks):
                lo = LANES * j
                sl = slice(lo, lo + LANES)
                energy_part = lax.dot_general(
                    c_ref[item, lo:, :], l_ref[item, 2 * lo:2 * lo + 2 * LANES, :], NT, preferred_element_type=f32
                )
                for i in range(j, blocks):
                    piece = energy_part[LANES * i - lo:LANES * (i + 1) - lo]
                    se_r, se_i = piece[:, :LANES], piece[:, LANES:]
                    cr, ci = brc[LANES * i:LANES * (i + 1)], bic[LANES * i:LANES * (i + 1)]
                    rr, ri = br[:, sl], bi[:, sl]
                    hr = cr * se_r - ci * se_i
                    hi = cr * se_i + ci * se_r
                    gr = hr * rr - hi * ri
                    gi = hr * ri + hi * rr
                    if i == j:
                        gr = gr + jnp.where(eye, rr, 0.0)
                        gi = gi + jnp.where(eye, ri, 0.0)
                        add_density(
                            s, j, -par_ref[item, 2, 0:1, :] * jnp.sum(jnp.where(eye, gi, 0.0), axis=0, keepdims=True)
                        )
                    gr, gi = gr.astype(bf16), gi.astype(bf16)
                    si = slice(LANES * i, LANES * (i + 1))
                    g_ref[item, si, 2 * lo:2 * lo + LANES] = gr
                    g_ref[item, si, 2 * lo + LANES:2 * lo + 2 * LANES] = gi
                    if i > j:
                        g_ref[item, sl, 2 * LANES * i:2 * LANES * i + LANES] = jnp.transpose(gr)
                        g_ref[item, sl, 2 * LANES * i + LANES:2 * LANES * (i + 1)] = jnp.transpose(gi)

        def slab(items, s, between=None):
            for item in items:
                couple(item, s)
            for item in items:
                left_product(item)
            if between is not None:
                between()
            for item in items:
                green(item, s)

        def own_piece(k):
            return w_ref.at[2 * k + c, rows(part * piece_at, part)]

        def send_row(k, d):
            to = place(x + (1 - c) * d, y + c * d, zl, c), e
            return remote(own_piece(k), own_piece(k), row_sems.at[0, k, d - 1], row_sems.at[1, k, d - 1], to)

        def send_plane(k, d):
            here = w_ref.at[2 * k + c, rows(part * 4 * b, 4 * part)]
            to = place(x + c * d, y + (1 - c) * d, zl, c), e
            return remote(here, here, plane_sems.at[0, k, d - 1], plane_sems.at[1, k, d - 1], to)

        def send_chip(k):
            here = w_ref.at[2 * k + c]
            return remote(here, here, chip_sems.at[0, k], chip_sems.at[1, k], (place(x, y, zl, 1 - c), e))

        def stage_row(k):
            @pl.when(k < pairs)
            def _():
                remote(own_piece(k), own_piece(k), z_send.at[0, 0], z_recv.at[k], (kt, 1)).wait_recv()
                for d in range(1, 4):
                    send_row(k, d).start()

        def stage_plane(k):
            @pl.when(k < pairs)
            def _():
                for d in range(1, 4):
                    send_row(k, d).wait_recv()
                for d in range(1, 4):
                    send_plane(k, d).start()

        def stage_chip(k):
            @pl.when(k < pairs)
            def _():
                for d in range(1, 4):
                    send_plane(k, d).wait_recv()
                send_chip(k).start()

        def stage_here(k):
            there = w_ref.at[2 * k + 1 - c]
            remote(there, there, chip_sems.at[0, k], chip_sems.at[1, k], (place(x, y, zl, 1 - c), e)).wait_recv()

        def send_line(group, first, count, d):
            pairs_sent = pl.ds(first, count)
            own = first - group * own_pairs
            return remote(
                den_ref.at[pairs_sent], line_in.at[spot, pl.ds(own, count)], line_send.at[first, d], line_recv.at[spot],
                (place(x, y, d // CORES, d % CORES), group),
            )

        def send_zone_line(d):
            return remote(
                den_ref.at[pl.ds(0, own_pairs)], line_in.at[spot], line_send.at[0, d], line_recv.at[spot], zone(d)
            )

        parcels = {3: (1, 2, 2), 5: (2, 4, 2), 6: (3, 6, 1), 7: (3, 7, 1)}

        first_slab(0)
        for i in range(1, slabs):
            for copy in loads(i):
                copy.wait()

        def alone(item):
            def step(s, carry):
                slab((item,), s)
                return carry

            return step

        lax.fori_loop(1, slabs, alone(0), 0)

        pl.semaphore_wait(barrier, PLANE - 1 + NZ * CORES - 1)
        mine = jnp.zeros((SUB, LANES), jnp.int32) + counts_ref[0]
        count_mine[0] = mine.astype(f32)

        def send_count(d):
            return remote(
                count_mine.at[0], count_in.at[xy], count_sems.at[0, d - 1], count_sems.at[1, d - 1], in_plane(d)
            )

        for d in range(1, PLANE):
            send_count(d).start()
        count_in[xy] = count_mine[0]
        stage_row(own_pairs)
        for d in range(1, PLANE):
            sender = ((x - d // NY + NX) % NX) * NY + (y - d % NY + NY) % NY
            remote(
                count_mine.at[0], count_in.at[sender], count_sems.at[0, d - 1], count_sems.at[1, d - 1], in_plane(d)
            ).wait_recv()
        here = spot * PLANE
        line = jnp.zeros((SUB, LANES), f32)
        for i in range(PLANE):
            line = line + jnp.where(lane == here + i, count_in[i], 0.0)
        count_mine[1] = line

        def send_zone(d):
            return remote(
                count_mine.at[1], count_all.at[spot], zone_sems.at[0, d - 1], zone_sems.at[1, d - 1], zone(d)
            )

        for d in range(1, NZ * CORES):
            send_zone(d).start()
        count_all[spot] = line
        stage_row(own_pairs + 1)
        stage_plane(own_pairs)
        for d in range(1, NZ * CORES):
            from_z, from_c = (zl - d // CORES + NZ) % NZ, (c + d) % CORES
            remote(
                count_mine.at[1], count_all.at[from_z * CORES + from_c], zone_sems.at[0, d - 1],
                zone_sems.at[1, d - 1], zone(d),
            ).wait_recv()
        every = count_all[0]
        for i in range(1, NZ * CORES):
            every = every + count_all[i]
        extra = every - 1.0
        upper = (
            lax.broadcasted_iota(jnp.int32, (LANES, LANES), 0) <= lax.broadcasted_iota(jnp.int32, (LANES, LANES), 1)
        )
        upto = jnp.dot(extra.astype(bf16), upper.astype(f32).astype(bf16), preferred_element_type=f32)
        before = upto - extra
        mine_f = (jnp.zeros((SUB, LANES), jnp.int32) + me).astype(f32)
        owner = jnp.logical_and(before <= mine_f, mine_f < upto)
        set_params(1, pick(owner, cosines), pick(owner, 1.0 + mine_f - before))
        first_slab(1)
        stage_plane(own_pairs + 1)
        slab((1,), 1)
        stage_row(own_pairs + 2)
        slab((1,), 2)
        stage_chip(own_pairs)
        stage_row(own_pairs + 3)
        slab((1,), 3)
        stage_row(own_pairs + 4)
        for d in range(1, NZ * CORES):
            send_zone_line(d).start()
        line_in[spot] = den_ref[:own_pairs]
        for run in range(1, EN):
            remote(tab_own, tab_ref.at[run], tab_sems.at[0], tab_sems.at[run], (kt, 0)).wait_recv()
        pl.semaphore_wait(ready_sem, (EN - 1) * NZ * CORES)
        stage_plane(own_pairs + 2)

        def both(k, carry):
            stage_here(k)
            stage_plane(k + 3)
            slab((0, 1), CORES * k, lambda: stage_chip(k + 1))
            stage_row(k + 5)
            slab((0, 1), CORES * k + 1)
            for last, parcel in parcels.items():
                @pl.when(k == last)
                def _():
                    for d in range(NZ * CORES):
                        send_line(*parcel, d).start()

            @pl.when(k == own_pairs + 2)
            def _():
                sum_line(1)

            return carry

        lax.fori_loop(own_pairs, pairs, both, 0)
        finish()

        for d in range(1, PLANE):
            send_count(d).wait_send()
        for d in range(1, NZ * CORES):
            send_zone(d).wait_send()
            send_zone_line(d).wait_send()

        def left(k, carry):
            for d in range(1, 4):
                send_row(k, d).wait_send()
                send_plane(k, d).wait_send()
            send_chip(k).wait_send()
            return carry

        lax.fori_loop(own_pairs, pairs, left, 0)
        for parcel in parcels.values():
            for d in range(NZ * CORES):
                send_line(*parcel, d).wait_send()


def body(counts, contact_slabs, onsite, hopping, potential_in, couple_base, couple_wave, doping, poisson_inverse):
    slabs, n = onsite.shape
    total = slabs * EN
    pairs = total // CORES
    vmem, anywhere = pl.BlockSpec(memory_space=pltpu.VMEM), pl.BlockSpec(memory_space=pl.ANY)
    tile = (SUB, LANES)
    sems = pltpu.SemaphoreType.DMA
    return pl.pallas_call(
        kernel,
        out_shape=(jax.ShapeDtypeStruct((slabs, n), f32), jax.ShapeDtypeStruct((slabs, n), f32)),
        in_specs=[anywhere] * 9,
        out_specs=(vmem, vmem),
        scratch_shapes=[
            pltpu.VMEM((total, 2 * n, n), bf16),
            pltpu.VMEM((EN, 2 * slabs, n), f32),
            pltpu.VMEM((2 * slabs, n), f32),
            pltpu.VMEM((3, slabs, n), f32),
            pltpu.VMEM((slabs, n), f32),
            pltpu.VMEM((n, n), f32),
            pltpu.SMEM((1,), jnp.int32),
            pltpu.SMEM((2,), jnp.int32),
            pltpu.VMEM((PLANE, *tile), f32),
            pltpu.VMEM((2, *tile), f32),
            pltpu.VMEM((NZ * CORES, *tile), f32),
            pltpu.VMEM((2, 3, *tile), f32),
            pltpu.VMEM((2, n, 2 * n), bf16),
            pltpu.VMEM((2, 2 * n, n), bf16),
            pltpu.VMEM((2, n, n), bf16),
            pltpu.VMEM((pairs, *tile), f32),
            pltpu.VMEM((NZ * CORES, slabs // CORES, *tile), f32),
            pltpu.VMEM((slabs // CORES, *tile), f32),
            pltpu.VMEM((PLANE, slabs // CORES, *tile), f32),
            sems((2, slabs)),
            sems((7,)),
            sems((EN,)),
            sems((2, PLANE - 1)),
            sems((2, NZ * CORES - 1)),
            sems((slabs // CORES, NZ)),
            sems((pairs,)),
            sems((2, pairs, 3)),
            sems((2, pairs, 3)),
            sems((2, pairs)),
            sems((pairs, NZ * CORES)),
            sems((NZ * CORES,)),
            sems((2, PLANE - 1)),
            pltpu.SemaphoreType.REGULAR,
        ],
        compiler_params=pltpu.CompilerParams(collective_id=0, has_side_effects=True, vmem_limit_bytes=62 * 2**20),
    )(counts, contact_slabs, onsite, hopping, potential_in, couple_base, couple_wave, doping, poisson_inverse)


def solution(mesh):
    return jax.shard_map(
        body,
        mesh=mesh,
        in_specs=(
            P("kt"), P(), P("en", None), P("en", None), P("en", None),
            P("en", None, None), P("en", None, None), P("en", None), P(),
        ),
        out_specs=(P("en", None), P("en", None)),
        check_vma=False,
    )
```

```python
import jax
import jax.numpy as jnp
from jax import lax
from jax.experimental import pallas as pl
from jax.experimental.pallas import tpu as pltpu
from jax.sharding import PartitionSpec as P

f32, bf16 = jnp.float32, jnp.bfloat16
NT = (((1,), (1,)), ((), ()))
NN = (((1,), (0,)), ((), ()))
MESH = pl.DeviceIdType.MESH

BOTTOM, GAP, FILLING, SPREAD = -1.0, 0.25, -0.5, 0.1
BROADENING, CONTACT = 1.0, 0.5
NX, NY, NZ, EN, CORES = 4, 4, 4, 4, 2
PLANE = NX * NY
LANES, SUB = 128, 8
SOURCES = ((4, (0, 1, 2, 3)), (8, (2, 3)), (11, (1, 0)), (15, (3, 2, 1, 0)))


def kernel(
    counts_in, contact_in, onsite_in, hopping_in, potential_in, base_ref, wave_ref, doping_in, inverse_in,
    den_out, pot_out,
    w_ref, tab_ref, tab_own, rows_ref, doping_ref, inverse_ref, counts_ref, contact_ref,
    count_in, count_mine, count_all, par_ref, g_ref, l_ref, c_ref, den_ref, line_in, line_ref, plane_in,
    load_sems, small_sems, tab_sems, count_sems, zone_sems, z_send, z_recv, row_sems, plane_sems, chip_sems,
    line_send, line_recv, sum_sems, ready_sem, plane_ready,
):
    kt, e = lax.axis_index("kt"), lax.axis_index("en")
    x, y, zl, c = kt // 32, (kt // 8) % 4, (kt // 2) % 4, kt % 2
    xy = x * NY + y
    slabs, n = base_ref.shape[0], base_ref.shape[-1]
    total = slabs * EN
    pairs, own_pairs = total // CORES, slabs // CORES
    blocks = n // LANES
    part = 2 * n // PLANE

    def place(x, y, zl, c):
        return (((x % NX) * NY + y % NY) * NZ + zl % NZ) * CORES + c % CORES

    def remote(src, dst, send, recv, where):
        return pltpu.make_async_remote_copy(src, dst, send, recv, device_id=where, device_id_type=MESH)

    def rows(first, count):
        return pl.ds(pl.multiple_of(first, 16), count)

    a, b = x + c * (y - x), y + c * (x - y)
    piece_at = 4 * b + a
    barrier = pltpu.get_barrier_semaphore()

    def in_plane(d):
        return place(x + d // NY, y + d % NY, zl, c), e

    def zone(d):
        return place(x, y, zl + d // CORES, c + d % CORES), e

    @pl.when(e == 0)
    def _():
        for run in range(1, EN):
            for d in range(NZ * CORES):
                pl.semaphore_signal(
                    barrier, 1, device_id=(place(x, y, d // CORES, d % CORES), run), device_id_type=MESH
                )

    small = [
        pltpu.make_async_copy(src, dst, small_sems.at[i])
        for i, (src, dst) in enumerate((
            (onsite_in, rows_ref.at[0]), (potential_in, rows_ref.at[1]), (hopping_in, rows_ref.at[2]),
            (doping_in, doping_ref), (inverse_in, inverse_ref), (counts_in, counts_ref), (contact_in, contact_ref),
        ))
    ]
    for copy in small:
        copy.start()

    spot = zl * CORES + c

    def signal_plane():
        for d in range(1, PLANE):
            pl.semaphore_signal(barrier, 1, device_id=in_plane(d), device_id_type=MESH)

    def send_plane_sum(d):
        return remote(line_ref, plane_in.at[xy], sum_sems.at[0, d - 1], sum_sems.at[1, d - 1], in_plane(d))

    def sum_line(first):
        for d in range(first, NZ * CORES):
            at = (spot + d) % (NZ * CORES)
            remote(line_ref, line_in.at[at], line_send.at[0, 0], line_recv.at[at], (kt, 0)).wait_recv()
        acc = line_in[0]
        for i in range(1, NZ * CORES):
            acc = acc + line_in[i]
        line_ref[...] = acc
        plane_in[xy] = acc
        for d in range(1, PLANE):
            send_plane_sum(d).start()

    def finish():
        for copy in small[3:5]:
            copy.wait()
        for d in range(1, PLANE):
            sender = ((x - d // NY + NX) % NX) * NY + (y - d % NY + NY) % NY
            remote(line_ref, plane_in.at[sender], sum_sems.at[0, d - 1], sum_sems.at[1, d - 1], in_plane(d)).wait_recv()
        acc = plane_in[0]
        for i in range(1, PLANE):
            acc = acc + plane_in[i]
        pot = jnp.zeros((slabs, n), f32)
        for j in range(blocks):
            sl = slice(LANES * j, LANES * (j + 1))
            block = jnp.concatenate(
                [acc[i // CORES, blocks * (i % CORES) + j:blocks * (i % CORES) + j + 1] for i in range(slabs)], axis=0
            )
            den_out[:, sl] = block
            pot = pot + lax.dot_general(
                block - doping_ref[:, sl], inverse_ref[:, sl], NT,
                precision=lax.Precision.HIGHEST, preferred_element_type=f32,
            )
        pot_out[...] = pot
        for d in range(1, PLANE):
            send_plane_sum(d).wait_send()

    def make_tab():
        for copy in small[:3]:
            copy.wait()
        tab_own[:slabs] = -rows_ref[0] - rows_ref[1]
        tab_own[slabs:] = rows_ref[2]

    def tab_copy(run):
        return remote(tab_own, tab_ref.at[run], tab_sems.at[0], tab_sems.at[run], (kt, 0))

    @pl.when(e != 0)
    def _():
        def fetch(i, first):
            index = piece_at if first else piece_at - PLANE // 2
            ref = base_ref if first else wave_ref
            return pltpu.make_async_copy(
                ref.at[2 * i + c, rows(part * index, part)],
                w_ref.at[2 * (e * own_pairs + i) + c, rows(part * piece_at, part)],
                load_sems.at[0, i],
            )

        for act in ("start", "wait"):
            for first in (True, False):
                in_half = (piece_at < PLANE // 2) if first else (piece_at >= PLANE // 2)

                @pl.when(in_half)
                def _():
                    for i in range(own_pairs):
                        getattr(fetch(i, first), act)()

            if act == "start":
                pl.semaphore_wait(barrier, NZ * CORES)

        def send_z(source, i, slot, to):
            k = source // NZ * own_pairs + i
            here = w_ref.at[2 * k + c, rows(part * piece_at, part)]
            return remote(here, here, z_send.at[i, slot], z_recv.at[k], (place(x, y, to, c), 0))

        def act_z(i, act):
            for source, targets in SOURCES:
                @pl.when(e * NZ + zl == source)
                def _():
                    for slot, to in enumerate(targets):
                        getattr(send_z(source, i, slot, to), act)()

        for i in range(own_pairs):
            act_z(i, "start")
        make_tab()
        tab_copy(e).start()
        for d in range(NZ * CORES):
            pl.semaphore_signal(
                ready_sem, 1, device_id=(place(x, y, d // CORES, d % CORES), 0), device_id_type=MESH
            )
        for i in range(own_pairs):
            act_z(i, "wait_send")

        tab_copy(e).wait_send()
        for copy in small[5:]:
            copy.wait()
        sum_line(0)
        finish()

    @pl.when(e == 0)
    def _():
        def loads(i):
            return (
                pltpu.make_async_copy(base_ref.at[i], w_ref.at[i, :n], load_sems.at[0, i]),
                pltpu.make_async_copy(wave_ref.at[i], w_ref.at[i, n:], load_sems.at[1, i]),
            )

        for i in range(1, slabs):
            for copy in loads(i):
                copy.start()
        signal_plane()
        for d in range(1, NZ * CORES):
            pl.semaphore_signal(barrier, 1, device_id=zone(d), device_id_type=MESH)

        lane = lax.broadcasted_iota(jnp.int32, (SUB, LANES), 1)
        momentum = (lane % PLANE) * (NZ * CORES) + lane // PLANE
        cosines = jnp.cos(jnp.pi * (momentum.astype(f32) + 0.5) / (PLANE * NZ * CORES))
        me = (zl * CORES + c) * PLANE + xy

        def set_params(item, cosine, j):
            energy = BOTTOM + GAP * j
            par_ref[item, 0] = cosine
            par_ref[item, 1] = energy
            par_ref[item, 2] = GAP / (1.0 + jnp.exp((energy - FILLING) / SPREAD)) / jnp.pi

        def pick(mask, values):
            return jnp.broadcast_to(jnp.sum(jnp.where(mask, values, 0.0), axis=1, keepdims=True), (SUB, LANES))

        set_params(0, pick(lane == me, cosines), jnp.zeros((SUB, LANES), f32))
        make_tab()
        tab_ref[0] = tab_own[...]
        for copy in small[5:]:
            copy.wait()
        den_ref[...] = jnp.zeros_like(den_ref)

        eye = lax.broadcasted_iota(jnp.int32, (LANES, LANES), 0) == lax.broadcasted_iota(jnp.int32, (LANES, LANES), 1)

        def wide(item, which):
            row = par_ref[item, which, 0:1, :]
            return jnp.concatenate([row] * blocks, axis=1)

        def inverse_diag(item, s):
            group, local = s // slabs, s % slabs
            touches = jnp.logical_or(contact_ref[0] == s, contact_ref[1] == s)
            di = BROADENING + CONTACT * touches.astype(f32)
            dr = (
                wide(item, 1) + tab_ref[group, pl.ds(local, 1), :]
                - wide(item, 0) * tab_ref[group, pl.ds(slabs + local, 1), :]
            )
            mag = dr * dr + di * di
            return dr / mag, -di / mag

        def add_density(s, j, value):
            at = pl.ds(blocks * (s % CORES) + j, 1)
            den_ref[s // CORES, at, :] = den_ref[s // CORES, at, :] + value

        def first_slab(item):
            g = g_ref.at[item]
            g[...] = jnp.zeros_like(g)
            br, bi = inverse_diag(item, 0)
            for i in range(blocks):
                sl = slice(LANES * i, LANES * (i + 1))
                g[sl, 2 * LANES * i:2 * LANES * i + LANES] = jnp.where(eye, br[:, sl], 0.0).astype(bf16)
                g[sl, 2 * LANES * i + LANES:2 * LANES * (i + 1)] = jnp.where(eye, bi[:, sl], 0.0).astype(bf16)
                add_density(0, i, -par_ref[item, 2, 0:1, :] * bi[:, sl])

        def couple(item, s):
            cosine = wide(item, 0)
            c_ref[item] = (w_ref[s, :n].astype(f32) + cosine * w_ref[s, n:].astype(f32)).astype(bf16)

        def left_product(item):
            for j in range(blocks):
                left = lax.dot_general(
                    c_ref[item], g_ref[item, :, 2 * LANES * j:2 * LANES * (j + 1)], NN, preferred_element_type=f32
                ).astype(bf16)
                sl = slice(LANES * j, LANES * (j + 1))
                for i in range(blocks):
                    piece = left[LANES * i:LANES * (i + 1)]
                    l_ref[item, 2 * LANES * i:2 * LANES * i + LANES, sl] = piece[:, :LANES]
                    l_ref[item, 2 * LANES * i + LANES:2 * LANES * (i + 1), sl] = piece[:, LANES:]

        def green(item, s):
            br, bi = inverse_diag(item, s)
            brc = jnp.transpose(jnp.broadcast_to(br, (LANES, n)))
            bic = jnp.transpose(jnp.broadcast_to(bi, (LANES, n)))
            for j in range(blocks):
                lo = LANES * j
                sl = slice(lo, lo + LANES)
                energy_part = lax.dot_general(
                    c_ref[item, lo:, :], l_ref[item, 2 * lo:2 * lo + 2 * LANES, :], NT, preferred_element_type=f32
                )
                for i in range(j, blocks):
                    piece = energy_part[LANES * i - lo:LANES * (i + 1) - lo]
                    se_r, se_i = piece[:, :LANES], piece[:, LANES:]
                    cr, ci = brc[LANES * i:LANES * (i + 1)], bic[LANES * i:LANES * (i + 1)]
                    rr, ri = br[:, sl], bi[:, sl]
                    hr = cr * se_r - ci * se_i
                    hi = cr * se_i + ci * se_r
                    gr = hr * rr - hi * ri
                    gi = hr * ri + hi * rr
                    if i == j:
                        gr = gr + jnp.where(eye, rr, 0.0)
                        gi = gi + jnp.where(eye, ri, 0.0)
                        add_density(
                            s, j, -par_ref[item, 2, 0:1, :] * jnp.sum(jnp.where(eye, gi, 0.0), axis=0, keepdims=True)
                        )
                    gr, gi = gr.astype(bf16), gi.astype(bf16)
                    si = slice(LANES * i, LANES * (i + 1))
                    g_ref[item, si, 2 * lo:2 * lo + LANES] = gr
                    g_ref[item, si, 2 * lo + LANES:2 * lo + 2 * LANES] = gi
                    if i > j:
                        g_ref[item, sl, 2 * LANES * i:2 * LANES * i + LANES] = jnp.transpose(gr)
                        g_ref[item, sl, 2 * LANES * i + LANES:2 * LANES * (i + 1)] = jnp.transpose(gi)

        def slab(items, s, between=None):
            for item in items:
                couple(item, s)
            for item in items:
                left_product(item)
            if between is not None:
                between()
            for item in items:
                green(item, s)

        def own_piece(k):
            return w_ref.at[2 * k + c, rows(part * piece_at, part)]

        def send_row(k, d):
            to = place(x + (1 - c) * d, y + c * d, zl, c), e
            return remote(own_piece(k), own_piece(k), row_sems.at[0, k, d - 1], row_sems.at[1, k, d - 1], to)

        def send_plane(k, d):
            here = w_ref.at[2 * k + c, rows(part * 4 * b, 4 * part)]
            to = place(x + c * d, y + (1 - c) * d, zl, c), e
            return remote(here, here, plane_sems.at[0, k, d - 1], plane_sems.at[1, k, d - 1], to)

        def send_chip(k):
            here = w_ref.at[2 * k + c]
            return remote(here, here, chip_sems.at[0, k], chip_sems.at[1, k], (place(x, y, zl, 1 - c), e))

        def stage_row(k):
            @pl.when(k < pairs)
            def _():
                remote(own_piece(k), own_piece(k), z_send.at[0, 0], z_recv.at[k], (kt, 1)).wait_recv()
                for d in (2, 1, 3):
                    send_row(k, d).start()

        def stage_plane(k):
            @pl.when(k < pairs)
            def _():
                for d in range(1, 4):
                    send_row(k, d).wait_recv()
                for d in (2, 1, 3):
                    send_plane(k, d).start()

        def stage_chip(k):
            @pl.when(k < pairs)
            def _():
                for d in range(1, 4):
                    send_plane(k, d).wait_recv()
                send_chip(k).start()

        def send_block(k, behind):
            here = w_ref.at[2 * k + c, rows(part * 4 * ((b + 4 - behind) % 4), 4 * part)]
            return remote(here, here, chip_sems.at[0, k], chip_sems.at[1, k], (place(x, y, zl, 1 - c), e))

        def stage_blocks(k):
            for d in (1, 3, 2):
                send_plane(k, d).wait_recv()
                send_block(k, d).start()

        def stage_here(k):
            there = w_ref.at[2 * k + 1 - c]
            remote(there, there, chip_sems.at[0, k], chip_sems.at[1, k], (place(x, y, zl, 1 - c), e)).wait_recv()

        def send_line(group, first, count, d):
            pairs_sent = pl.ds(first, count)
            own = first - group * own_pairs
            return remote(
                den_ref.at[pairs_sent], line_in.at[spot, pl.ds(own, count)], line_send.at[first, d], line_recv.at[spot],
                (place(x, y, d // CORES, d % CORES), group),
            )

        def send_zone_line(d):
            return remote(
                den_ref.at[pl.ds(0, own_pairs)], line_in.at[spot], line_send.at[0, d], line_recv.at[spot], zone(d)
            )

        parcels = {3: (1, 2, 2), 5: (2, 4, 2), 6: (3, 6, 1), 7: (3, 7, 1)}

        first_slab(0)
        for i in range(1, slabs):
            for copy in loads(i):
                copy.wait()

        def alone(item):
            def step(s, carry):
                slab((item,), s)
                return carry

            return step

        lax.fori_loop(1, slabs, alone(0), 0)

        pl.semaphore_wait(barrier, PLANE - 1 + NZ * CORES - 1)
        mine = jnp.zeros((SUB, LANES), jnp.int32) + counts_ref[0]
        count_mine[0] = mine.astype(f32)

        def send_count(d):
            return remote(
                count_mine.at[0], count_in.at[xy], count_sems.at[0, d - 1], count_sems.at[1, d - 1], in_plane(d)
            )

        for d in range(1, PLANE):
            send_count(d).start()
        count_in[xy] = count_mine[0]
        stage_row(own_pairs)
        for d in range(1, PLANE):
            sender = ((x - d // NY + NX) % NX) * NY + (y - d % NY + NY) % NY
            remote(
                count_mine.at[0], count_in.at[sender], count_sems.at[0, d - 1], count_sems.at[1, d - 1], in_plane(d)
            ).wait_recv()
        here = spot * PLANE
        line = jnp.zeros((SUB, LANES), f32)
        for i in range(PLANE):
            line = line + jnp.where(lane == here + i, count_in[i], 0.0)
        count_mine[1] = line

        def send_zone(d):
            return remote(
                count_mine.at[1], count_all.at[spot], zone_sems.at[0, d - 1], zone_sems.at[1, d - 1], zone(d)
            )

        for d in range(1, NZ * CORES):
            send_zone(d).start()
        count_all[spot] = line
        stage_row(own_pairs + 1)
        stage_plane(own_pairs)
        send_block(own_pairs, 0).start()
        for d in range(1, NZ * CORES):
            from_z, from_c = (zl - d // CORES + NZ) % NZ, (c + d) % CORES
            remote(
                count_mine.at[1], count_all.at[from_z * CORES + from_c], zone_sems.at[0, d - 1],
                zone_sems.at[1, d - 1], zone(d),
            ).wait_recv()
        every = count_all[0]
        for i in range(1, NZ * CORES):
            every = every + count_all[i]
        extra = every - 1.0
        upper = (
            lax.broadcasted_iota(jnp.int32, (LANES, LANES), 0) <= lax.broadcasted_iota(jnp.int32, (LANES, LANES), 1)
        )
        upto = jnp.dot(extra.astype(bf16), upper.astype(f32).astype(bf16), preferred_element_type=f32)
        before = upto - extra
        mine_f = (jnp.zeros((SUB, LANES), jnp.int32) + me).astype(f32)
        owner = jnp.logical_and(before <= mine_f, mine_f < upto)
        set_params(1, pick(owner, cosines), pick(owner, 1.0 + mine_f - before))
        first_slab(1)
        stage_plane(own_pairs + 1)
        slab((1,), 1)
        stage_row(own_pairs + 2)
        slab((1,), 2)
        stage_blocks(own_pairs)
        stage_row(own_pairs + 3)
        slab((1,), 3)
        stage_row(own_pairs + 4)
        for d in range(1, NZ * CORES):
            send_zone_line(d).start()
        line_in[spot] = den_ref[:own_pairs]
        for run in range(1, EN):
            remote(tab_own, tab_ref.at[run], tab_sems.at[0], tab_sems.at[run], (kt, 0)).wait_recv()
        pl.semaphore_wait(ready_sem, (EN - 1) * NZ * CORES)
        for d in range(1, PLANE):
            pl.semaphore_signal(plane_ready, 1, device_id=in_plane(d), device_id_type=MESH)
        stage_plane(own_pairs + 2)

        def both(k, carry):
            stage_here(k)
            stage_plane(k + 3)
            slab((0, 1), CORES * k, lambda: stage_chip(k + 1))
            stage_row(k + 5)
            slab((0, 1), CORES * k + 1)
            @pl.when(k == own_pairs)
            def _():
                pl.semaphore_wait(plane_ready, PLANE - 1)

            for last, parcel in parcels.items():
                @pl.when(k == last)
                def _():
                    for d in range(NZ * CORES):
                        send_line(*parcel, d).start()

            @pl.when(k == own_pairs + 2)
            def _():
                sum_line(1)

            return carry

        lax.fori_loop(own_pairs, pairs, both, 0)
        finish()

        for d in range(1, PLANE):
            send_count(d).wait_send()
        for d in range(1, NZ * CORES):
            send_zone(d).wait_send()
            send_zone_line(d).wait_send()

        def left(k, carry):
            for d in range(1, 4):
                send_row(k, d).wait_send()
                send_plane(k, d).wait_send()
            send_chip(k).wait_send()
            return carry

        lax.fori_loop(own_pairs, pairs, left, 0)
        for parcel in parcels.values():
            for d in range(NZ * CORES):
                send_line(*parcel, d).wait_send()


def body(counts, contact_slabs, onsite, hopping, potential_in, couple_base, couple_wave, doping, poisson_inverse):
    slabs, n = onsite.shape
    total = slabs * EN
    pairs = total // CORES
    vmem, anywhere = pl.BlockSpec(memory_space=pltpu.VMEM), pl.BlockSpec(memory_space=pl.ANY)
    tile = (SUB, LANES)
    sems = pltpu.SemaphoreType.DMA
    return pl.pallas_call(
        kernel,
        out_shape=(jax.ShapeDtypeStruct((slabs, n), f32), jax.ShapeDtypeStruct((slabs, n), f32)),
        in_specs=[anywhere] * 9,
        out_specs=(vmem, vmem),
        scratch_shapes=[
            pltpu.VMEM((total, 2 * n, n), bf16),
            pltpu.VMEM((EN, 2 * slabs, n), f32),
            pltpu.VMEM((2 * slabs, n), f32),
            pltpu.VMEM((3, slabs, n), f32),
            pltpu.VMEM((slabs, n), f32),
            pltpu.VMEM((n, n), f32),
            pltpu.SMEM((1,), jnp.int32),
            pltpu.SMEM((2,), jnp.int32),
            pltpu.VMEM((PLANE, *tile), f32),
            pltpu.VMEM((2, *tile), f32),
            pltpu.VMEM((NZ * CORES, *tile), f32),
            pltpu.VMEM((2, 3, *tile), f32),
            pltpu.VMEM((2, n, 2 * n), bf16),
            pltpu.VMEM((2, 2 * n, n), bf16),
            pltpu.VMEM((2, n, n), bf16),
            pltpu.VMEM((pairs, *tile), f32),
            pltpu.VMEM((NZ * CORES, slabs // CORES, *tile), f32),
            pltpu.VMEM((slabs // CORES, *tile), f32),
            pltpu.VMEM((PLANE, slabs // CORES, *tile), f32),
            sems((2, slabs)),
            sems((7,)),
            sems((EN,)),
            sems((2, PLANE - 1)),
            sems((2, NZ * CORES - 1)),
            sems((slabs // CORES, NZ)),
            sems((pairs,)),
            sems((2, pairs, 3)),
            sems((2, pairs, 3)),
            sems((2, pairs)),
            sems((pairs, NZ * CORES)),
            sems((NZ * CORES,)),
            sems((2, PLANE - 1)),
            pltpu.SemaphoreType.REGULAR,
            pltpu.SemaphoreType.REGULAR,
        ],
        compiler_params=pltpu.CompilerParams(collective_id=0, has_side_effects=True, vmem_limit_bytes=62 * 2**20),
    )(counts, contact_slabs, onsite, hopping, potential_in, couple_base, couple_wave, doping, poisson_inverse)


def solution(mesh):
    return jax.shard_map(
        body,
        mesh=mesh,
        in_specs=(
            P("kt"), P(), P("en", None), P("en", None), P("en", None),
            P("en", None, None), P("en", None, None), P("en", None), P(),
        ),
        out_specs=(P("en", None), P("en", None)),
        check_vma=False,
    )
```

```python
import jax
import jax.numpy as jnp
from jax import lax
from jax.experimental import pallas as pl
from jax.experimental.pallas import tpu as pltpu
from jax.sharding import PartitionSpec as P

f32, bf16 = jnp.float32, jnp.bfloat16
NT = (((1,), (1,)), ((), ()))
NN = (((1,), (0,)), ((), ()))
MESH = pl.DeviceIdType.MESH

BOTTOM, GAP, FILLING, SPREAD = -1.0, 0.25, -0.5, 0.1
BROADENING, CONTACT = 1.0, 0.5
NX, NY, NZ, EN, CORES = 4, 4, 4, 4, 2
PLANE = NX * NY
LANES, SUB = 128, 8
SOURCES = ((4, (0, 1, 2, 3)), (8, (2, 3)), (11, (1, 0)), (15, (3, 2, 1, 0)))


def kernel(
    counts_in, contact_in, onsite_in, hopping_in, potential_in, base_ref, wave_ref, doping_in, inverse_in,
    out_ref,
    w_ref, tab_ref, tab_own, rows_ref, doping_ref, inverse_ref, counts_ref, contact_ref,
    count_in, count_mine, count_all, par_ref, g_ref, l_ref, c_ref, den_ref, line_in, line_ref, plane_in,
    load_sems, small_sems, tab_sems, count_sems, zone_sems, z_send, z_recv, row_sems, plane_sems, chip_sems,
    line_send, line_recv, sum_sems, ready_sem, plane_ready,
):
    kt, e = lax.axis_index("kt"), lax.axis_index("en")
    x, y, zl, c = kt // 32, (kt // 8) % 4, (kt // 2) % 4, kt % 2
    xy = x * NY + y
    slabs, n = base_ref.shape[0], base_ref.shape[-1]
    total = slabs * EN
    pairs, own_pairs = total // CORES, slabs // CORES
    blocks = n // LANES
    part = 2 * n // PLANE

    def place(x, y, zl, c):
        return (((x % NX) * NY + y % NY) * NZ + zl % NZ) * CORES + c % CORES

    def remote(src, dst, send, recv, where):
        return pltpu.make_async_remote_copy(src, dst, send, recv, device_id=where, device_id_type=MESH)

    def rows(first, count):
        return pl.ds(pl.multiple_of(first, 16), count)

    a, b = x + c * (y - x), y + c * (x - y)
    piece_at = 4 * b + a
    barrier = pltpu.get_barrier_semaphore()

    def in_plane(d):
        return place(x + d // NY, y + d % NY, zl, c), e

    def zone(d):
        return place(x, y, zl + d // CORES, c + d % CORES), e

    @pl.when(e == 0)
    def _():
        for run in range(1, EN):
            for d in range(NZ * CORES):
                pl.semaphore_signal(
                    barrier, 1, device_id=(place(x, y, d // CORES, d % CORES), run), device_id_type=MESH
                )

    small = [
        pltpu.make_async_copy(src, dst, small_sems.at[i])
        for i, (src, dst) in enumerate((
            (onsite_in, rows_ref.at[0]), (potential_in, rows_ref.at[1]), (hopping_in, rows_ref.at[2]),
            (doping_in, doping_ref), (inverse_in, inverse_ref), (counts_in, counts_ref), (contact_in, contact_ref),
        ))
    ]
    for copy in small:
        copy.start()

    spot = zl * CORES + c

    def signal_plane():
        for d in range(1, PLANE):
            pl.semaphore_signal(barrier, 1, device_id=in_plane(d), device_id_type=MESH)

    def send_plane_sum(d):
        return remote(line_ref, plane_in.at[xy], sum_sems.at[0, d - 1], sum_sems.at[1, d - 1], in_plane(d))

    def sum_line(first):
        for d in range(first, NZ * CORES):
            at = (spot + d) % (NZ * CORES)
            remote(line_ref, line_in.at[at], line_send.at[0, 0], line_recv.at[at], (kt, 0)).wait_recv()
        acc = line_in[0]
        for i in range(1, NZ * CORES):
            acc = acc + line_in[i]
        line_ref[...] = acc
        plane_in[xy] = acc
        for d in range(1, PLANE):
            send_plane_sum(d).start()

    def finish():
        for copy in small[3:5]:
            copy.wait()
        for d in range(1, PLANE):
            sender = ((x - d // NY + NX) % NX) * NY + (y - d % NY + NY) % NY
            remote(line_ref, plane_in.at[sender], sum_sems.at[0, d - 1], sum_sems.at[1, d - 1], in_plane(d)).wait_recv()
        acc = plane_in[0]
        for i in range(1, PLANE):
            acc = acc + plane_in[i]
        pot = jnp.zeros((slabs, n), f32)
        for j in range(blocks):
            sl = slice(LANES * j, LANES * (j + 1))
            block = jnp.concatenate(
                [acc[i // CORES, blocks * (i % CORES) + j:blocks * (i % CORES) + j + 1] for i in range(slabs)], axis=0
            )
            out_ref[:slabs, sl] = block
            pot = pot + lax.dot_general(
                block - doping_ref[:, sl], inverse_ref[:, sl], NT,
                precision=lax.Precision.HIGHEST, preferred_element_type=f32,
            )
        out_ref[slabs:] = pot
        for d in range(1, PLANE):
            send_plane_sum(d).wait_send()

    def make_tab():
        for copy in small[:3]:
            copy.wait()
        tab_own[:slabs] = -rows_ref[0] - rows_ref[1]
        tab_own[slabs:] = rows_ref[2]

    def tab_copy(run):
        return remote(tab_own, tab_ref.at[run], tab_sems.at[0], tab_sems.at[run], (kt, 0))

    @pl.when(e != 0)
    def _():
        def fetch(i, first):
            index = piece_at if first else piece_at - PLANE // 2
            ref = base_ref if first else wave_ref
            return pltpu.make_async_copy(
                ref.at[2 * i + c, rows(part * index, part)],
                w_ref.at[2 * (e * own_pairs + i) + c, rows(part * piece_at, part)],
                load_sems.at[0, i],
            )

        for act in ("start", "wait"):
            for first in (True, False):
                in_half = (piece_at < PLANE // 2) if first else (piece_at >= PLANE // 2)

                @pl.when(in_half)
                def _():
                    for i in range(own_pairs):
                        getattr(fetch(i, first), act)()

            if act == "start":
                pl.semaphore_wait(barrier, NZ * CORES)

        def send_z(source, i, slot, to):
            k = source // NZ * own_pairs + i
            here = w_ref.at[2 * k + c, rows(part * piece_at, part)]
            return remote(here, here, z_send.at[i, slot], z_recv.at[k], (place(x, y, to, c), 0))

        def act_z(i, act):
            for source, targets in SOURCES:
                @pl.when(e * NZ + zl == source)
                def _():
                    for slot, to in enumerate(targets):
                        getattr(send_z(source, i, slot, to), act)()

        act_z(0, "start")
        make_tab()
        tab_copy(e).start()
        for d in range(NZ * CORES):
            pl.semaphore_signal(
                ready_sem, 1, device_id=(place(x, y, d // CORES, d % CORES), 0), device_id_type=MESH
            )
        for i in range(own_pairs):
            act_z(i, "wait_send")
            if i + 1 < own_pairs:
                act_z(i + 1, "start")


        tab_copy(e).wait_send()
        for copy in small[5:]:
            copy.wait()
        sum_line(0)
        finish()

    @pl.when(e == 0)
    def _():
        def loads(i):
            return (
                pltpu.make_async_copy(base_ref.at[i], w_ref.at[i, :n], load_sems.at[0, i]),
                pltpu.make_async_copy(wave_ref.at[i], w_ref.at[i, n:], load_sems.at[1, i]),
            )

        for i in range(1, slabs):
            for copy in loads(i):
                copy.start()
        signal_plane()
        for d in range(1, NZ * CORES):
            pl.semaphore_signal(barrier, 1, device_id=zone(d), device_id_type=MESH)

        lane = lax.broadcasted_iota(jnp.int32, (SUB, LANES), 1)
        momentum = (lane % PLANE) * (NZ * CORES) + lane // PLANE
        cosines = jnp.cos(jnp.pi * (momentum.astype(f32) + 0.5) / (PLANE * NZ * CORES))
        me = (zl * CORES + c) * PLANE + xy

        def set_params(item, cosine, j):
            energy = BOTTOM + GAP * j
            par_ref[item, 0] = cosine
            par_ref[item, 1] = energy
            par_ref[item, 2] = GAP / (1.0 + jnp.exp((energy - FILLING) / SPREAD)) / jnp.pi

        def pick(mask, values):
            return jnp.broadcast_to(jnp.sum(jnp.where(mask, values, 0.0), axis=1, keepdims=True), (SUB, LANES))

        set_params(0, pick(lane == me, cosines), jnp.zeros((SUB, LANES), f32))
        make_tab()
        tab_ref[0] = tab_own[...]
        for copy in small[5:]:
            copy.wait()
        den_ref[...] = jnp.zeros_like(den_ref)

        eye = lax.broadcasted_iota(jnp.int32, (LANES, LANES), 0) == lax.broadcasted_iota(jnp.int32, (LANES, LANES), 1)

        def wide(item, which):
            row = par_ref[item, which, 0:1, :]
            return jnp.concatenate([row] * blocks, axis=1)

        def inverse_diag(item, s):
            group, local = s // slabs, s % slabs
            touches = jnp.logical_or(contact_ref[0] == s, contact_ref[1] == s)
            di = BROADENING + CONTACT * touches.astype(f32)
            dr = (
                wide(item, 1) + tab_ref[group, pl.ds(local, 1), :]
                - wide(item, 0) * tab_ref[group, pl.ds(slabs + local, 1), :]
            )
            mag = dr * dr + di * di
            return dr / mag, -di / mag

        def add_density(s, j, value):
            at = pl.ds(blocks * (s % CORES) + j, 1)
            den_ref[s // CORES, at, :] = den_ref[s // CORES, at, :] + value

        def first_slab(item):
            g = g_ref.at[item]
            g[...] = jnp.zeros_like(g)
            br, bi = inverse_diag(item, 0)
            for i in range(blocks):
                sl = slice(LANES * i, LANES * (i + 1))
                g[sl, 2 * LANES * i:2 * LANES * i + LANES] = jnp.where(eye, br[:, sl], 0.0).astype(bf16)
                g[sl, 2 * LANES * i + LANES:2 * LANES * (i + 1)] = jnp.where(eye, bi[:, sl], 0.0).astype(bf16)
                add_density(0, i, -par_ref[item, 2, 0:1, :] * bi[:, sl])

        def couple(item, s):
            cosine = wide(item, 0)
            c_ref[item] = (w_ref[s, :n].astype(f32) + cosine * w_ref[s, n:].astype(f32)).astype(bf16)

        def left_product(item):
            for j in range(blocks):
                left = lax.dot_general(
                    c_ref[item], g_ref[item, :, 2 * LANES * j:2 * LANES * (j + 1)], NN, preferred_element_type=f32
                ).astype(bf16)
                sl = slice(LANES * j, LANES * (j + 1))
                for i in range(blocks):
                    piece = left[LANES * i:LANES * (i + 1)]
                    l_ref[item, 2 * LANES * i:2 * LANES * i + LANES, sl] = piece[:, :LANES]
                    l_ref[item, 2 * LANES * i + LANES:2 * LANES * (i + 1), sl] = piece[:, LANES:]

        def green(item, s):
            br, bi = inverse_diag(item, s)
            brc = jnp.transpose(jnp.broadcast_to(br, (LANES, n)))
            bic = jnp.transpose(jnp.broadcast_to(bi, (LANES, n)))
            for j in range(blocks):
                lo = LANES * j
                sl = slice(lo, lo + LANES)
                energy_part = lax.dot_general(
                    c_ref[item, lo:, :], l_ref[item, 2 * lo:2 * lo + 2 * LANES, :], NT, preferred_element_type=f32
                )
                for i in range(j, blocks):
                    piece = energy_part[LANES * i - lo:LANES * (i + 1) - lo]
                    se_r, se_i = piece[:, :LANES], piece[:, LANES:]
                    cr, ci = brc[LANES * i:LANES * (i + 1)], bic[LANES * i:LANES * (i + 1)]
                    rr, ri = br[:, sl], bi[:, sl]
                    hr = cr * se_r - ci * se_i
                    hi = cr * se_i + ci * se_r
                    gr = hr * rr - hi * ri
                    gi = hr * ri + hi * rr
                    if i == j:
                        gr = gr + jnp.where(eye, rr, 0.0)
                        gi = gi + jnp.where(eye, ri, 0.0)
                        add_density(
                            s, j, -par_ref[item, 2, 0:1, :] * jnp.sum(jnp.where(eye, gi, 0.0), axis=0, keepdims=True)
                        )
                    gr, gi = gr.astype(bf16), gi.astype(bf16)
                    si = slice(LANES * i, LANES * (i + 1))
                    g_ref[item, si, 2 * lo:2 * lo + LANES] = gr
                    g_ref[item, si, 2 * lo + LANES:2 * lo + 2 * LANES] = gi
                    if i > j:
                        g_ref[item, sl, 2 * LANES * i:2 * LANES * i + LANES] = jnp.transpose(gr)
                        g_ref[item, sl, 2 * LANES * i + LANES:2 * LANES * (i + 1)] = jnp.transpose(gi)

        def slab(items, s, between=None):
            for item in items:
                couple(item, s)
            for item in items:
                left_product(item)
            if between is not None:
                between()
            for item in items:
                green(item, s)

        def own_piece(k):
            return w_ref.at[2 * k + c, rows(part * piece_at, part)]

        def send_row(k, d):
            to = place(x + (1 - c) * d, y + c * d, zl, c), e
            return remote(own_piece(k), own_piece(k), row_sems.at[0, k, d - 1], row_sems.at[1, k, d - 1], to)

        def send_plane(k, d):
            here = w_ref.at[2 * k + c, rows(part * 4 * b, 4 * part)]
            to = place(x + c * d, y + (1 - c) * d, zl, c), e
            return remote(here, here, plane_sems.at[0, k, d - 1], plane_sems.at[1, k, d - 1], to)

        def send_chip(k):
            here = w_ref.at[2 * k + c]
            return remote(here, here, chip_sems.at[0, k], chip_sems.at[1, k], (place(x, y, zl, 1 - c), e))

        def stage_row(k):
            @pl.when(k < pairs)
            def _():
                remote(own_piece(k), own_piece(k), z_send.at[0, 0], z_recv.at[k], (kt, 1)).wait_recv()
                for d in (2, 1, 3):
                    send_row(k, d).start()

        def stage_plane(k):
            @pl.when(k < pairs)
            def _():
                for d in range(1, 4):
                    send_row(k, d).wait_recv()
                for d in (2, 1, 3):
                    send_plane(k, d).start()

        def stage_chip(k):
            @pl.when(k < pairs)
            def _():
                for d in range(1, 4):
                    send_plane(k, d).wait_recv()
                send_chip(k).start()

        def send_block(k, behind):
            here = w_ref.at[2 * k + c, rows(part * 4 * ((b + 4 - behind) % 4), 4 * part)]
            return remote(here, here, chip_sems.at[0, k], chip_sems.at[1, k], (place(x, y, zl, 1 - c), e))

        def stage_blocks(k):
            for d in (1, 3, 2):
                send_plane(k, d).wait_recv()
                send_block(k, d).start()

        def stage_here(k):
            there = w_ref.at[2 * k + 1 - c]
            remote(there, there, chip_sems.at[0, k], chip_sems.at[1, k], (place(x, y, zl, 1 - c), e)).wait_recv()

        def send_line(group, first, count, d):
            pairs_sent = pl.ds(first, count)
            own = first - group * own_pairs
            return remote(
                den_ref.at[pairs_sent], line_in.at[spot, pl.ds(own, count)], line_send.at[first, d], line_recv.at[spot],
                (place(x, y, d // CORES, d % CORES), group),
            )

        def send_zone_line(d):
            return remote(
                den_ref.at[pl.ds(0, own_pairs)], line_in.at[spot], line_send.at[0, d], line_recv.at[spot], zone(d)
            )

        parcels = {3: (1, 2, 2), 5: (2, 4, 2), 6: (3, 6, 1), 7: (3, 7, 1)}

        first_slab(0)
        for i in range(1, slabs):
            for copy in loads(i):
                copy.wait()

        def alone(item):
            def step(s, carry):
                slab((item,), s)
                return carry

            return step

        lax.fori_loop(1, slabs, alone(0), 0)

        pl.semaphore_wait(barrier, PLANE - 1 + NZ * CORES - 1)
        mine = jnp.zeros((SUB, LANES), jnp.int32) + counts_ref[0]
        count_mine[0] = mine.astype(f32)

        def send_count(d):
            return remote(
                count_mine.at[0], count_in.at[xy], count_sems.at[0, d - 1], count_sems.at[1, d - 1], in_plane(d)
            )

        for d in range(1, PLANE):
            send_count(d).start()
        count_in[xy] = count_mine[0]
        for d in range(1, PLANE):
            sender = ((x - d // NY + NX) % NX) * NY + (y - d % NY + NY) % NY
            remote(
                count_mine.at[0], count_in.at[sender], count_sems.at[0, d - 1], count_sems.at[1, d - 1], in_plane(d)
            ).wait_recv()
        here = spot * PLANE
        line = jnp.zeros((SUB, LANES), f32)
        for i in range(PLANE):
            line = line + jnp.where(lane == here + i, count_in[i], 0.0)
        count_mine[1] = line

        def send_zone(d):
            return remote(
                count_mine.at[1], count_all.at[spot], zone_sems.at[0, d - 1], zone_sems.at[1, d - 1], zone(d)
            )

        for d in range(1, NZ * CORES):
            send_zone(d).start()
        count_all[spot] = line
        stage_row(own_pairs)
        stage_row(own_pairs + 1)
        stage_plane(own_pairs)
        send_block(own_pairs, 0).start()
        for d in range(1, NZ * CORES):
            from_z, from_c = (zl - d // CORES + NZ) % NZ, (c + d) % CORES
            remote(
                count_mine.at[1], count_all.at[from_z * CORES + from_c], zone_sems.at[0, d - 1],
                zone_sems.at[1, d - 1], zone(d),
            ).wait_recv()
        every = count_all[0]
        for i in range(1, NZ * CORES):
            every = every + count_all[i]
        extra = every - 1.0
        upper = (
            lax.broadcasted_iota(jnp.int32, (LANES, LANES), 0) <= lax.broadcasted_iota(jnp.int32, (LANES, LANES), 1)
        )
        upto = jnp.dot(extra.astype(bf16), upper.astype(f32).astype(bf16), preferred_element_type=f32)
        before = upto - extra
        mine_f = (jnp.zeros((SUB, LANES), jnp.int32) + me).astype(f32)
        owner = jnp.logical_and(before <= mine_f, mine_f < upto)
        set_params(1, pick(owner, cosines), pick(owner, 1.0 + mine_f - before))
        first_slab(1)
        stage_plane(own_pairs + 1)
        slab((1,), 1)
        stage_row(own_pairs + 2)
        slab((1,), 2)
        stage_blocks(own_pairs)
        stage_row(own_pairs + 3)
        slab((1,), 3)
        stage_row(own_pairs + 4)
        for d in range(1, NZ * CORES):
            send_zone_line(d).start()
        line_in[spot] = den_ref[:own_pairs]
        for run in range(1, EN):
            remote(tab_own, tab_ref.at[run], tab_sems.at[0], tab_sems.at[run], (kt, 0)).wait_recv()
        pl.semaphore_wait(ready_sem, (EN - 1) * NZ * CORES)
        for d in range(1, PLANE):
            pl.semaphore_signal(plane_ready, 1, device_id=in_plane(d), device_id_type=MESH)
        stage_plane(own_pairs + 2)

        def both(k, carry):
            stage_here(k)
            stage_plane(k + 3)
            slab((0, 1), CORES * k, lambda: stage_chip(k + 1))
            stage_row(k + 5)
            slab((0, 1), CORES * k + 1)
            @pl.when(k == own_pairs)
            def _():
                pl.semaphore_wait(plane_ready, PLANE - 1)

            for last, parcel in parcels.items():
                @pl.when(k == last)
                def _():
                    for d in range(NZ * CORES):
                        send_line(*parcel, d).start()

            @pl.when(k == own_pairs + 2)
            def _():
                sum_line(1)

            return carry

        lax.fori_loop(own_pairs, pairs, both, 0)
        finish()

        for d in range(1, PLANE):
            send_count(d).wait_send()
        for d in range(1, NZ * CORES):
            send_zone(d).wait_send()
            send_zone_line(d).wait_send()

        def left(k, carry):
            for d in range(1, 4):
                send_row(k, d).wait_send()
                send_plane(k, d).wait_send()
            send_chip(k).wait_send()
            return carry

        lax.fori_loop(own_pairs, pairs, left, 0)
        for parcel in parcels.values():
            for d in range(NZ * CORES):
                send_line(*parcel, d).wait_send()


def body(counts, contact_slabs, onsite, hopping, potential_in, couple_base, couple_wave, doping, poisson_inverse):
    slabs, n = onsite.shape
    total = slabs * EN
    pairs = total // CORES
    vmem, anywhere = pl.BlockSpec(memory_space=pltpu.VMEM), pl.BlockSpec(memory_space=pl.ANY)
    tile = (SUB, LANES)
    sems = pltpu.SemaphoreType.DMA
    out = pl.pallas_call(
        kernel,
        out_shape=jax.ShapeDtypeStruct((2 * slabs, n), f32),
        in_specs=[anywhere] * 9,
        out_specs=vmem,
        scratch_shapes=[
            pltpu.VMEM((total, 2 * n, n), bf16),
            pltpu.VMEM((EN, 2 * slabs, n), f32),
            pltpu.VMEM((2 * slabs, n), f32),
            pltpu.VMEM((3, slabs, n), f32),
            pltpu.VMEM((slabs, n), f32),
            pltpu.VMEM((n, n), f32),
            pltpu.SMEM((1,), jnp.int32),
            pltpu.SMEM((2,), jnp.int32),
            pltpu.VMEM((PLANE, *tile), f32),
            pltpu.VMEM((2, *tile), f32),
            pltpu.VMEM((NZ * CORES, *tile), f32),
            pltpu.VMEM((2, 3, *tile), f32),
            pltpu.VMEM((2, n, 2 * n), bf16),
            pltpu.VMEM((2, 2 * n, n), bf16),
            pltpu.VMEM((2, n, n), bf16),
            pltpu.VMEM((pairs, *tile), f32),
            pltpu.VMEM((NZ * CORES, slabs // CORES, *tile), f32),
            pltpu.VMEM((slabs // CORES, *tile), f32),
            pltpu.VMEM((PLANE, slabs // CORES, *tile), f32),
            sems((2, slabs)),
            sems((7,)),
            sems((EN,)),
            sems((2, PLANE - 1)),
            sems((2, NZ * CORES - 1)),
            sems((slabs // CORES, NZ)),
            sems((pairs,)),
            sems((2, pairs, 3)),
            sems((2, pairs, 3)),
            sems((2, pairs)),
            sems((pairs, NZ * CORES)),
            sems((NZ * CORES,)),
            sems((2, PLANE - 1)),
            pltpu.SemaphoreType.REGULAR,
            pltpu.SemaphoreType.REGULAR,
        ],
        compiler_params=pltpu.CompilerParams(collective_id=0, has_side_effects=True, vmem_limit_bytes=62 * 2**20),
    )(counts, contact_slabs, onsite, hopping, potential_in, couple_base, couple_wave, doping, poisson_inverse)
    return out[:slabs], out[slabs:]


def solution(mesh):
    return jax.shard_map(
        body,
        mesh=mesh,
        in_specs=(
            P("kt"), P(), P("en", None), P("en", None), P("en", None),
            P("en", None, None), P("en", None, None), P("en", None), P(),
        ),
        out_specs=(P("en", None), P("en", None)),
        check_vma=False,
    )
```

```python
import jax
import jax.numpy as jnp
from jax import lax
from jax.experimental import pallas as pl
from jax.experimental.pallas import tpu as pltpu
from jax.sharding import PartitionSpec as P

f32, bf16 = jnp.float32, jnp.bfloat16
NT = (((1,), (1,)), ((), ()))
NN = (((1,), (0,)), ((), ()))
MESH = pl.DeviceIdType.MESH

BOTTOM, GAP, FILLING, SPREAD = -1.0, 0.25, -0.5, 0.1
BROADENING, CONTACT = 1.0, 0.5
NX, NY, NZ, EN, CORES = 4, 4, 4, 4, 2
PLANE = NX * NY
LANES, SUB = 128, 8
SOURCES = ((4, (0, 1, 2, 3)), (8, (2, 3)), (11, (1, 0)), (15, (3, 2, 1, 0)))


def kernel(
    counts_in, contact_in, onsite_in, hopping_in, potential_in, base_ref, wave_ref, doping_in, inverse_in,
    out_ref,
    w_ref, tab_ref, tab_own, rows_ref, doping_ref, inverse_ref, counts_ref, contact_ref,
    count_in, count_mine, count_all, par_ref, g_ref, l_ref, c_ref, den_ref, line_in, line_ref, plane_in,
    load_sems, small_sems, tab_sems, count_sems, zone_sems, z_send, z_recv, row_sems, plane_sems, chip_sems,
    line_send, line_recv, sum_sems, ready_sem, plane_ready,
):
    kt, e = lax.axis_index("kt"), lax.axis_index("en")
    x, y, zl, c = kt // 32, (kt // 8) % 4, (kt // 2) % 4, kt % 2
    xy = x * NY + y
    slabs, n = base_ref.shape[0], base_ref.shape[-1]
    total = slabs * EN
    pairs, own_pairs = total // CORES, slabs // CORES
    blocks = n // LANES
    part = 2 * n // PLANE

    def place(x, y, zl, c):
        return (((x % NX) * NY + y % NY) * NZ + zl % NZ) * CORES + c % CORES

    def remote(src, dst, send, recv, where):
        return pltpu.make_async_remote_copy(src, dst, send, recv, device_id=where, device_id_type=MESH)

    def rows(first, count):
        return pl.ds(pl.multiple_of(first, 16), count)

    a, b = x + c * (y - x), y + c * (x - y)
    piece_at = 4 * b + a
    barrier = pltpu.get_barrier_semaphore()

    def in_plane(d):
        return place(x + d // NY, y + d % NY, zl, c), e

    def zone(d):
        return place(x, y, zl + d // CORES, c + d % CORES), e

    @pl.when(e == 0)
    def _():
        for run in range(1, EN):
            for d in range(NZ * CORES):
                pl.semaphore_signal(
                    barrier, 1, device_id=(place(x, y, d // CORES, d % CORES), run), device_id_type=MESH
                )

    small = [
        pltpu.make_async_copy(src, dst, small_sems.at[i])
        for i, (src, dst) in enumerate((
            (onsite_in, rows_ref.at[0]), (potential_in, rows_ref.at[1]), (hopping_in, rows_ref.at[2]),
            (doping_in, doping_ref), (inverse_in, inverse_ref), (counts_in, counts_ref), (contact_in, contact_ref),
        ))
    ]
    for copy in small:
        copy.start()

    spot = zl * CORES + c

    def signal_plane():
        for d in range(1, PLANE):
            pl.semaphore_signal(barrier, 1, device_id=in_plane(d), device_id_type=MESH)

    def send_plane_sum(d):
        return remote(line_ref, plane_in.at[xy], sum_sems.at[0, d - 1], sum_sems.at[1, d - 1], in_plane(d))

    def sum_line(first):
        for d in range(first, NZ * CORES):
            at = (spot + d) % (NZ * CORES)
            remote(line_ref, line_in.at[at], line_send.at[0, 0], line_recv.at[at], (kt, 0)).wait_recv()
        acc = line_in[0]
        for i in range(1, NZ * CORES):
            acc = acc + line_in[i]
        line_ref[...] = acc
        plane_in[xy] = acc
        for d in range(1, PLANE):
            send_plane_sum(d).start()

    def finish():
        for copy in small[3:5]:
            copy.wait()
        for d in range(1, PLANE):
            sender = ((x - d // NY + NX) % NX) * NY + (y - d % NY + NY) % NY
            remote(line_ref, plane_in.at[sender], sum_sems.at[0, d - 1], sum_sems.at[1, d - 1], in_plane(d)).wait_recv()
        acc = plane_in[0]
        for i in range(1, PLANE):
            acc = acc + plane_in[i]
        pot = jnp.zeros((slabs, n), f32)
        for j in range(blocks):
            sl = slice(LANES * j, LANES * (j + 1))
            block = jnp.concatenate(
                [acc[i // CORES, blocks * (i % CORES) + j:blocks * (i % CORES) + j + 1] for i in range(slabs)], axis=0
            )
            out_ref[:slabs, sl] = block
            pot = pot + lax.dot_general(
                block - doping_ref[:, sl], inverse_ref[:, sl], NT,
                precision=lax.Precision.HIGHEST, preferred_element_type=f32,
            )
        out_ref[slabs:] = pot
        for d in range(1, PLANE):
            send_plane_sum(d).wait_send()

    def make_tab():
        for copy in small[:3]:
            copy.wait()
        tab_own[:slabs] = -rows_ref[0] - rows_ref[1]
        tab_own[slabs:] = rows_ref[2]

    def tab_copy(run):
        return remote(tab_own, tab_ref.at[run], tab_sems.at[0], tab_sems.at[run], (kt, 0))

    @pl.when(e != 0)
    def _():
        def fetch(i, first):
            index = piece_at if first else piece_at - PLANE // 2
            ref = base_ref if first else wave_ref
            return pltpu.make_async_copy(
                ref.at[2 * i + c, rows(part * index, part)],
                w_ref.at[2 * (e * own_pairs + i) + c, rows(part * piece_at, part)],
                load_sems.at[0, i],
            )

        for act in ("start", "wait"):
            for first in (True, False):
                in_half = (piece_at < PLANE // 2) if first else (piece_at >= PLANE // 2)

                @pl.when(in_half)
                def _():
                    for i in range(own_pairs):
                        getattr(fetch(i, first), act)()

            if act == "start":
                pl.semaphore_wait(barrier, NZ * CORES)

        def send_z(source, i, slot, to):
            k = source // NZ * own_pairs + i
            here = w_ref.at[2 * k + c, rows(part * piece_at, part)]
            return remote(here, here, z_send.at[i, slot], z_recv.at[k], (place(x, y, to, c), 0))

        def act_z(i, act):
            for source, targets in SOURCES:
                @pl.when(e * NZ + zl == source)
                def _():
                    for slot, to in enumerate(targets):
                        getattr(send_z(source, i, slot, to), act)()

        act_z(0, "start")
        make_tab()
        tab_copy(e).start()
        for d in range(NZ * CORES):
            pl.semaphore_signal(
                ready_sem, 1, device_id=(place(x, y, d // CORES, d % CORES), 0), device_id_type=MESH
            )
        for i in range(own_pairs):
            act_z(i, "wait_send")
            if i + 1 < own_pairs:
                act_z(i + 1, "start")


        tab_copy(e).wait_send()
        for copy in small[5:]:
            copy.wait()
        sum_line(0)
        finish()

    @pl.when(e == 0)
    def _():
        def loads(i):
            return (
                pltpu.make_async_copy(base_ref.at[i], w_ref.at[i, :n], load_sems.at[0, i]),
                pltpu.make_async_copy(wave_ref.at[i], w_ref.at[i, n:], load_sems.at[1, i]),
            )

        for i in range(1, slabs):
            for copy in loads(i):
                copy.start()
        signal_plane()
        for d in range(1, NZ * CORES):
            pl.semaphore_signal(barrier, 1, device_id=zone(d), device_id_type=MESH)

        lane = lax.broadcasted_iota(jnp.int32, (SUB, LANES), 1)
        momentum = (lane % PLANE) * (NZ * CORES) + lane // PLANE
        cosines = jnp.cos(jnp.pi * (momentum.astype(f32) + 0.5) / (PLANE * NZ * CORES))
        me = (zl * CORES + c) * PLANE + xy

        def set_params(item, cosine, j):
            energy = BOTTOM + GAP * j
            par_ref[item, 0] = cosine
            par_ref[item, 1] = energy
            par_ref[item, 2] = GAP / (1.0 + jnp.exp((energy - FILLING) / SPREAD)) / jnp.pi

        def pick(mask, values):
            return jnp.broadcast_to(jnp.sum(jnp.where(mask, values, 0.0), axis=1, keepdims=True), (SUB, LANES))

        set_params(0, pick(lane == me, cosines), jnp.zeros((SUB, LANES), f32))
        make_tab()
        tab_ref[0] = tab_own[...]
        for copy in small[5:]:
            copy.wait()
        den_ref[...] = jnp.zeros_like(den_ref)

        eye = lax.broadcasted_iota(jnp.int32, (LANES, LANES), 0) == lax.broadcasted_iota(jnp.int32, (LANES, LANES), 1)

        def wide(item, which):
            row = par_ref[item, which, 0:1, :]
            return jnp.concatenate([row] * blocks, axis=1)

        def inverse_diag(item, s):
            group, local = s // slabs, s % slabs
            touches = jnp.logical_or(contact_ref[0] == s, contact_ref[1] == s)
            di = BROADENING + CONTACT * touches.astype(f32)
            dr = (
                wide(item, 1) + tab_ref[group, pl.ds(local, 1), :]
                - wide(item, 0) * tab_ref[group, pl.ds(slabs + local, 1), :]
            )
            mag = dr * dr + di * di
            return dr / mag, -di / mag

        def add_density(s, j, value):
            at = pl.ds(blocks * (s % CORES) + j, 1)
            den_ref[s // CORES, at, :] = den_ref[s // CORES, at, :] + value

        def first_slab(item):
            g = g_ref.at[item]
            g[...] = jnp.zeros_like(g)
            br, bi = inverse_diag(item, 0)
            for i in range(blocks):
                sl = slice(LANES * i, LANES * (i + 1))
                g[sl, 2 * LANES * i:2 * LANES * i + LANES] = jnp.where(eye, br[:, sl], 0.0).astype(bf16)
                g[sl, 2 * LANES * i + LANES:2 * LANES * (i + 1)] = jnp.where(eye, bi[:, sl], 0.0).astype(bf16)
                add_density(0, i, -par_ref[item, 2, 0:1, :] * bi[:, sl])

        def couple(item, s):
            cosine = wide(item, 0)
            c_ref[item] = (w_ref[s, :n].astype(f32) + cosine * w_ref[s, n:].astype(f32)).astype(bf16)

        def left_product(item):
            for j in range(blocks):
                left = lax.dot_general(
                    c_ref[item], g_ref[item, :, 2 * LANES * j:2 * LANES * (j + 1)], NN, preferred_element_type=f32
                ).astype(bf16)
                sl = slice(LANES * j, LANES * (j + 1))
                for i in range(blocks):
                    piece = left[LANES * i:LANES * (i + 1)]
                    l_ref[item, 2 * LANES * i:2 * LANES * i + LANES, sl] = piece[:, :LANES]
                    l_ref[item, 2 * LANES * i + LANES:2 * LANES * (i + 1), sl] = piece[:, LANES:]

        def green(item, s, last=False):
            br, bi = inverse_diag(item, s)
            brc = jnp.transpose(jnp.broadcast_to(br, (LANES, n)))
            bic = jnp.transpose(jnp.broadcast_to(bi, (LANES, n)))
            for j in range(blocks):
                lo = LANES * j
                sl = slice(lo, lo + LANES)
                end = j + 1 if last else blocks
                energy_part = lax.dot_general(
                    c_ref[item, lo:LANES * end, :], l_ref[item, 2 * lo:2 * lo + 2 * LANES, :], NT, preferred_element_type=f32
                )
                for i in range(j, end):
                    piece = energy_part[LANES * i - lo:LANES * (i + 1) - lo]
                    se_r, se_i = piece[:, :LANES], piece[:, LANES:]
                    cr, ci = brc[LANES * i:LANES * (i + 1)], bic[LANES * i:LANES * (i + 1)]
                    rr, ri = br[:, sl], bi[:, sl]
                    hr = cr * se_r - ci * se_i
                    hi = cr * se_i + ci * se_r
                    gr = hr * rr - hi * ri
                    gi = hr * ri + hi * rr
                    if i == j:
                        gr = gr + jnp.where(eye, rr, 0.0)
                        gi = gi + jnp.where(eye, ri, 0.0)
                        add_density(
                            s, j, -par_ref[item, 2, 0:1, :] * jnp.sum(jnp.where(eye, gi, 0.0), axis=0, keepdims=True)
                        )
                    if last:
                        continue
                    gr, gi = gr.astype(bf16), gi.astype(bf16)
                    si = slice(LANES * i, LANES * (i + 1))
                    g_ref[item, si, 2 * lo:2 * lo + LANES] = gr
                    g_ref[item, si, 2 * lo + LANES:2 * lo + 2 * LANES] = gi
                    if i > j:
                        g_ref[item, sl, 2 * LANES * i:2 * LANES * i + LANES] = jnp.transpose(gr)
                        g_ref[item, sl, 2 * LANES * i + LANES:2 * LANES * (i + 1)] = jnp.transpose(gi)

        def slab(items, s, between=None, last=False):
            for item in items:
                couple(item, s)
            for item in items:
                left_product(item)
            if between is not None:
                between()
            for item in items:
                green(item, s, last)

        def own_piece(k):
            return w_ref.at[2 * k + c, rows(part * piece_at, part)]

        def send_row(k, d):
            to = place(x + (1 - c) * d, y + c * d, zl, c), e
            return remote(own_piece(k), own_piece(k), row_sems.at[0, k, d - 1], row_sems.at[1, k, d - 1], to)

        def send_plane(k, d):
            here = w_ref.at[2 * k + c, rows(part * 4 * b, 4 * part)]
            to = place(x + c * d, y + (1 - c) * d, zl, c), e
            return remote(here, here, plane_sems.at[0, k, d - 1], plane_sems.at[1, k, d - 1], to)

        def send_chip(k):
            here = w_ref.at[2 * k + c]
            return remote(here, here, chip_sems.at[0, k], chip_sems.at[1, k], (place(x, y, zl, 1 - c), e))

        def stage_row(k):
            @pl.when(k < pairs)
            def _():
                remote(own_piece(k), own_piece(k), z_send.at[0, 0], z_recv.at[k], (kt, 1)).wait_recv()
                for d in (2, 1, 3):
                    send_row(k, d).start()

        def stage_plane(k):
            @pl.when(k < pairs)
            def _():
                for d in range(1, 4):
                    send_row(k, d).wait_recv()
                for d in (2, 1, 3):
                    send_plane(k, d).start()

        def stage_chip(k):
            @pl.when(k < pairs)
            def _():
                for d in range(1, 4):
                    send_plane(k, d).wait_recv()
                send_chip(k).start()

        def send_block(k, behind):
            here = w_ref.at[2 * k + c, rows(part * 4 * ((b + 4 - behind) % 4), 4 * part)]
            return remote(here, here, chip_sems.at[0, k], chip_sems.at[1, k], (place(x, y, zl, 1 - c), e))

        def stage_blocks(k):
            for d in (1, 3, 2):
                send_plane(k, d).wait_recv()
                send_block(k, d).start()

        def stage_here(k):
            there = w_ref.at[2 * k + 1 - c]
            remote(there, there, chip_sems.at[0, k], chip_sems.at[1, k], (place(x, y, zl, 1 - c), e)).wait_recv()

        def send_line(group, first, count, d):
            pairs_sent = pl.ds(first, count)
            own = first - group * own_pairs
            return remote(
                den_ref.at[pairs_sent], line_in.at[spot, pl.ds(own, count)], line_send.at[first, d], line_recv.at[spot],
                (place(x, y, d // CORES, d % CORES), group),
            )

        def send_zone_line(d):
            return remote(
                den_ref.at[pl.ds(0, own_pairs)], line_in.at[spot], line_send.at[0, d], line_recv.at[spot], zone(d)
            )

        parcels = {3: (1, 2, 2), 5: (2, 4, 2), 6: (3, 6, 1), 7: (3, 7, 1)}

        first_slab(0)
        for i in range(1, slabs):
            for copy in loads(i):
                copy.wait()

        def alone(item):
            def step(s, carry):
                slab((item,), s)
                return carry

            return step

        lax.fori_loop(1, slabs, alone(0), 0)

        pl.semaphore_wait(barrier, PLANE - 1 + NZ * CORES - 1)
        count_mine[0] = counts_ref[...]

        def send_count(d):
            return remote(
                count_mine.at[0], count_in.at[xy], count_sems.at[0, d - 1], count_sems.at[1, d - 1], in_plane(d)
            )

        for d in range(1, PLANE):
            send_count(d).start()
        count_in[xy] = count_mine[0]
        for d in range(1, PLANE):
            sender = ((x - d // NY + NX) % NX) * NY + (y - d % NY + NY) % NY
            remote(
                count_mine.at[0], count_in.at[sender], count_sems.at[0, d - 1], count_sems.at[1, d - 1], in_plane(d)
            ).wait_recv()
        here = spot * PLANE
        line = jnp.zeros((SUB, LANES), f32)
        for i in range(PLANE):
            line = line + jnp.where(lane == here + i, count_in[i], 0.0)
        count_mine[1] = line

        def send_zone(d):
            return remote(
                count_mine.at[1], count_all.at[spot], zone_sems.at[0, d - 1], zone_sems.at[1, d - 1], zone(d)
            )

        for d in range(1, NZ * CORES):
            send_zone(d).start()
        count_all[spot] = line
        stage_row(own_pairs)
        stage_row(own_pairs + 1)
        stage_plane(own_pairs)
        send_block(own_pairs, 0).start()
        for d in range(1, NZ * CORES):
            from_z, from_c = (zl - d // CORES + NZ) % NZ, (c + d) % CORES
            remote(
                count_mine.at[1], count_all.at[from_z * CORES + from_c], zone_sems.at[0, d - 1],
                zone_sems.at[1, d - 1], zone(d),
            ).wait_recv()
        every = count_all[0]
        for i in range(1, NZ * CORES):
            every = every + count_all[i]
        extra = every - 1.0
        upper = (
            lax.broadcasted_iota(jnp.int32, (LANES, LANES), 0) <= lax.broadcasted_iota(jnp.int32, (LANES, LANES), 1)
        )
        upto = jnp.dot(extra.astype(bf16), upper.astype(f32).astype(bf16), preferred_element_type=f32)
        before = upto - extra
        mine_f = (jnp.zeros((SUB, LANES), jnp.int32) + me).astype(f32)
        owner = jnp.logical_and(before <= mine_f, mine_f < upto)
        set_params(1, pick(owner, cosines), pick(owner, 1.0 + mine_f - before))
        first_slab(1)
        stage_plane(own_pairs + 1)
        slab((1,), 1)
        stage_row(own_pairs + 2)
        slab((1,), 2)
        stage_blocks(own_pairs)
        stage_row(own_pairs + 3)
        slab((1,), 3)
        stage_row(own_pairs + 4)
        for d in range(1, NZ * CORES):
            send_zone_line(d).start()
        line_in[spot] = den_ref[:own_pairs]
        for run in range(1, EN):
            remote(tab_own, tab_ref.at[run], tab_sems.at[0], tab_sems.at[run], (kt, 0)).wait_recv()
        pl.semaphore_wait(ready_sem, (EN - 1) * NZ * CORES)
        for d in range(1, PLANE):
            pl.semaphore_signal(plane_ready, 1, device_id=in_plane(d), device_id_type=MESH)
        stage_plane(own_pairs + 2)

        def both(k, carry, last=False):
            stage_here(k)
            stage_plane(k + 3)
            slab((0, 1), CORES * k, lambda: stage_chip(k + 1))
            stage_row(k + 5)
            slab((0, 1), CORES * k + 1, last=last)
            @pl.when(k == own_pairs)
            def _():
                pl.semaphore_wait(plane_ready, PLANE - 1)

            for last, parcel in parcels.items():
                @pl.when(k == last)
                def _():
                    for d in range(NZ * CORES):
                        send_line(*parcel, d).start()

            @pl.when(k == own_pairs + 2)
            def _():
                sum_line(1)

            return carry

        lax.fori_loop(own_pairs, pairs - 1, both, 0)
        both(pairs - 1, 0, True)
        finish()

        for d in range(1, PLANE):
            send_count(d).wait_send()
        for d in range(1, NZ * CORES):
            send_zone(d).wait_send()
            send_zone_line(d).wait_send()

        def left(k, carry):
            for d in range(1, 4):
                send_row(k, d).wait_send()
                send_plane(k, d).wait_send()
            send_chip(k).wait_send()
            return carry

        lax.fori_loop(own_pairs, pairs, left, 0)
        for parcel in parcels.values():
            for d in range(NZ * CORES):
                send_line(*parcel, d).wait_send()


def body(counts, contact_slabs, onsite, hopping, potential_in, couple_base, couple_wave, doping, poisson_inverse):
    slabs, n = onsite.shape
    total = slabs * EN
    pairs = total // CORES
    vmem, anywhere = pl.BlockSpec(memory_space=pltpu.VMEM), pl.BlockSpec(memory_space=pl.ANY)
    tile = (SUB, LANES)
    sems = pltpu.SemaphoreType.DMA
    out = pl.pallas_call(
        kernel,
        out_shape=jax.ShapeDtypeStruct((2 * slabs, n), f32),
        in_specs=[anywhere] * 9,
        out_specs=vmem,
        scratch_shapes=[
            pltpu.VMEM((total, 2 * n, n), bf16),
            pltpu.VMEM((EN, 2 * slabs, n), f32),
            pltpu.VMEM((2 * slabs, n), f32),
            pltpu.VMEM((3, slabs, n), f32),
            pltpu.VMEM((slabs, n), f32),
            pltpu.VMEM((n, n), f32),
            pltpu.VMEM(tile, f32),
            pltpu.SMEM((2,), jnp.int32),
            pltpu.VMEM((PLANE, *tile), f32),
            pltpu.VMEM((2, *tile), f32),
            pltpu.VMEM((NZ * CORES, *tile), f32),
            pltpu.VMEM((2, 3, *tile), f32),
            pltpu.VMEM((2, n, 2 * n), bf16),
            pltpu.VMEM((2, 2 * n, n), bf16),
            pltpu.VMEM((2, n, n), bf16),
            pltpu.VMEM((pairs, *tile), f32),
            pltpu.VMEM((NZ * CORES, slabs // CORES, *tile), f32),
            pltpu.VMEM((slabs // CORES, *tile), f32),
            pltpu.VMEM((PLANE, slabs // CORES, *tile), f32),
            sems((2, slabs)),
            sems((7,)),
            sems((EN,)),
            sems((2, PLANE - 1)),
            sems((2, NZ * CORES - 1)),
            sems((slabs // CORES, NZ)),
            sems((pairs,)),
            sems((2, pairs, 3)),
            sems((2, pairs, 3)),
            sems((2, pairs)),
            sems((pairs, NZ * CORES)),
            sems((NZ * CORES,)),
            sems((2, PLANE - 1)),
            pltpu.SemaphoreType.REGULAR,
            pltpu.SemaphoreType.REGULAR,
        ],
        compiler_params=pltpu.CompilerParams(collective_id=0, has_side_effects=True, vmem_limit_bytes=62 * 2**20),
    )(jnp.broadcast_to(counts.astype(f32).reshape(1, 1), tile), contact_slabs, onsite, hopping, potential_in, couple_base, couple_wave, doping, poisson_inverse)
    return out[:slabs], out[slabs:]


def solution(mesh):
    return jax.shard_map(
        body,
        mesh=mesh,
        in_specs=(
            P("kt"), P(), P("en", None), P("en", None), P("en", None),
            P("en", None, None), P("en", None, None), P("en", None), P(),
        ),
        out_specs=(P("en", None), P("en", None)),
        check_vma=False,
    )
```
